32 devices in a mesh: groups: 2 (over y), plane: 4 (over z), normal: 2 (over x), inner: 2 (over core).
Axes of the slice: x: 2, y: 2, z: 4, core: 2. Of those that a mesh axis runs over, the one named last changes fastest.
Arguments:
- phase: int32 [64, 64, 256], P(('groups', 'normal'), 'plane', 'inner'), parts along dimension 0, may hold values 0 or 1
- velocity: float32 [3, 64, 64, 256], P(None, ('groups', 'normal'), 'plane', 'inner'), parts along dimension 1, may hold values from -0.75 to 0.75
- stress: float32 [6, 64, 64, 256], P(None, ('groups', 'normal'), 'plane', 'inner'), parts along dimension 1, may hold values from -0.2 to 0.2
- new_slot: int32 [128], P(('groups', 'plane')), parts along dimension 0, may hold values from 0 to 63, as said below
Outputs:
- moved: bfloat16 [10, 64, 64, 256], P(None, ('groups', 'normal'), 'plane', 'inner'), parts along dimension 1
The draws below stay inside these ranges and needn't reach their ends.
There are 2 independent parts, one for each index of `groups`. The reference program is written for one: setup_inputs(seed, part) draws one part's arguments, and reference() takes and returns one part's arrays. A program takes and returns all parts, laid end to end along the dimension named above; each array names one. Nothing has to cross between parts.
Inputs may be any that keep to these rules, and one draw needn't show every extreme that they name: `new_slot`: a permutation of 0 to 63; of the 16 column blocks held by one plane device, at most 4 go to any one plane device, and exactly 4 do in every draw.
All inputs are finite; a program needn't handle non-finite values. No bound on the sum of `phase` on one device may be relied on, other than what follows from the above.
Results may differ from the reference program's by a relative error of at most 0.003.
Values may be sent and summed in bfloat16 or wider, within the bound.
A program may use at most 64 MiB of HBM per device.

```python
import jax
import jax.numpy as jnp
from jax import lax

CX = 16
STEPS = 2
NZ = 32
NX = 64
NY = 256


def draw_new_slot(key, part):
    key = jax.random.fold_in(key, 7)
    planes = NX // CX
    first_key, second_key = jax.random.split(key)
    offsets = jax.random.permutation(first_key, planes)
    rotation = jax.random.randint(second_key, (planes,), 0, CX)
    blocks = jnp.arange(NX, dtype=jnp.int32)
    source = blocks // CX
    within = blocks % CX
    target = (source + offsets[within // 2 % planes]) % planes
    return (target * CX + (within + rotation[target]) % CX).astype(jnp.int32)


def touch_ends(array, stream_key, smallest, top_value):
    index_at = [jax.random.randint(jax.random.fold_in(stream_key, axis), (), 0, length) for axis, length in enumerate(array.shape)]
    longest = array.shape.index(max(array.shape))
    beside = index_at[:longest] + [(index_at[longest] + 1) % array.shape[longest]] + index_at[longest + 1:]
    return array.at[tuple(index_at)].set(smallest).at[tuple(beside)].set(top_value)


def level_of(own_key, dims, cuts, smallest, largest):
    def one(dim, blocks):
        heights = jax.random.uniform(jax.random.fold_in(jax.random.fold_in(own_key, 6), dim), (blocks,), jnp.float32, smallest / len(cuts), largest / len(cuts))
        return jnp.repeat(jnp.exp(heights), dims[dim] // blocks).reshape((-1,) + (1,) * (len(dims) - dim - 1))

    gain = one(*cuts[0])
    for cut in cuts[1:]:
        gain = gain * one(*cut)
    return gain


def bell_draw(rng, shape, deviation, most, cuts=(), kind=jnp.bfloat16):
    values = deviation * jax.random.normal(rng, shape, jnp.float32)
    if cuts:
        values = values * level_of(rng, shape, cuts, -0.22, 0.18)
    return jnp.clip(values, -most, most).astype(kind)


def setup_inputs(seed: int = 0, part: int = 0) -> dict:
    arg_keys = jax.random.split(jax.random.key(seed), 5)
    part_keys = jax.random.split(jax.random.fold_in(arg_keys[4], part), 5)
    phase = touch_ends((jax.random.randint(part_keys[0], (NZ, NX, NY), 0, 2) < 1).astype(jnp.int32), jax.random.fold_in(part_keys[0], 1), 0, 1)
    velocity = bell_draw(part_keys[1], (3, NZ, NX, NY), 0.05, 0.75, ((1, 2), (2, 4), (3, 2)), jnp.float32)
    stress = bell_draw(part_keys[2], (6, NZ, NX, NY), 0.05, 0.2, ((1, 2), (2, 4), (3, 2)), jnp.float32)
    new_slot = draw_new_slot(jax.random.fold_in(jax.random.fold_in(arg_keys[4], part), 71), part)
    return {"phase": phase, "velocity": velocity, "stress": stress, "new_slot": new_slot}


lattice_vectors = ((0, 0, 0), (1, 0, 0), (-1, 0, 0), (0, 1, 0), (0, -1, 0), (0, 0, 1), (0, 0, -1), (1, 1, 0), (1, -1, 0), (-1, 1, 0), (-1, -1, 0), (1, 0, 1), (1, 0, -1), (-1, 0, 1), (-1, 0, -1), (0, 1, 1), (0, 1, -1), (0, -1, 1), (0, -1, -1))
lattice_weights = (1.0 / 3.0,) + (1.0 / 18.0,) * 6 + (1.0 / 36.0,) * 12
pair_list = ((0, 0), (1, 1), (2, 2), (0, 1), (0, 2), (1, 2))
keep_rate = 0.375
coupling = 1.5


def build_population():
    table = []
    for index_v in range(19):
        vector = lattice_vectors[index_v]
        weight = lattice_weights[index_v]
        row = [weight]
        for axis_a in range(3):
            row.append(3.0 * weight * vector[axis_a])
        for axis_a, axis_b in pair_list:
            if axis_a == axis_b:
                row.append(4.5 * weight * (vector[axis_a] * vector[axis_a] - 1.0 / 3.0))
            else:
                row.append(9.0 * weight * vector[axis_a] * vector[axis_b])
        table.append(row)
    return table


def build_moments():
    table = [[1.0] * 19]
    for axis_a in range(3):
        table.append([float(lattice_vectors[index_v][axis_a]) for index_v in range(19)])
    for axis_a, axis_b in pair_list:
        table.append([float(lattice_vectors[index_v][axis_a] * lattice_vectors[index_v][axis_b]) for index_v in range(19)])
    return table


def initial(phase, velocity, stress):
    density = jnp.where(phase == 1, 2.0, 0.3).astype(jnp.float32)
    momentum = density[None] * velocity
    parts = [density, momentum[0], momentum[1], momentum[2]]
    for index_k, (axis_a, axis_b) in enumerate(pair_list):
        second = momentum[axis_a] * momentum[axis_b] / density + stress[index_k]
        if axis_a == axis_b:
            second = second + density / 3.0
        parts.append(second)
    return jnp.stack(parts)


def force_from(potential_pad, lead, extent):
    s_z, s_x, s_y = extent
    center = potential_pad[lead:lead + s_z, lead:lead + s_x, lead:lead + s_y]
    sums = [jnp.zeros(center.shape, jnp.float32) for axis_a in range(3)]
    for index_v in range(1, 19):
        shift_z, shift_x, shift_y = lattice_vectors[index_v]
        neighbour = potential_pad[lead + shift_z:lead + shift_z + s_z, lead + shift_x:lead + shift_x + s_x, lead + shift_y:lead + shift_y + s_y]
        for axis_a in range(3):
            factor = lattice_weights[index_v] * lattice_vectors[index_v][axis_a]
            if factor != 0.0:
                sums[axis_a] = sums[axis_a] + factor * neighbour
    return jnp.stack([coupling * center * partial_sum for partial_sum in sums])


def collide(moments, force):
    density = moments[0]
    momentum = moments[1:4]
    parts = [density, momentum[0] + force[0], momentum[1] + force[1], momentum[2] + force[2]]
    for index_k, (axis_a, axis_b) in enumerate(pair_list):
        balance = momentum[axis_a] * momentum[axis_b] / density
        if axis_a == axis_b:
            balance = balance + density / 3.0
        relaxed = balance + keep_rate * (moments[4 + index_k] - balance)
        relaxed = relaxed + (momentum[axis_a] * force[axis_b] + force[axis_a] * momentum[axis_b]) / density
        if axis_a == axis_b:
            relaxed = relaxed - density / 3.0
        parts.append(relaxed)
    return jnp.stack(parts)


def stream(post_pad, extent):
    s_z, s_x, s_y = extent
    spread = jnp.einsum("ik,kzxy->izxy", jnp.asarray(build_population(), dtype=jnp.float32), post_pad, precision=lax.Precision.HIGHEST)
    shifted = []
    for index_v in range(19):
        shift_z, shift_x, shift_y = lattice_vectors[index_v]
        shifted.append(spread[index_v, 1 - shift_z:1 - shift_z + s_z, 1 - shift_x:1 - shift_x + s_x, 1 - shift_y:1 - shift_y + s_y])
    stacked = jnp.stack(shifted)
    return jnp.einsum("ki,izxy->kzxy", jnp.asarray(build_moments(), dtype=jnp.float32), stacked, precision=lax.Precision.HIGHEST)


def reference(phase, velocity, stress, new_slot):
    moments = initial(phase, velocity, stress)
    extent = phase.shape
    for step_index in range(STEPS):
        potential = 1.0 - jnp.exp(-moments[0])
        padded = jnp.pad(potential, 1, mode="wrap")
        force = force_from(padded, 1, extent)
        post = collide(moments, force)
        post_pad = jnp.pad(post, ((0, 0), (1, 1), (1, 1), (1, 1)), mode="wrap")
        moments = stream(post_pad, extent)
    rounded = moments.astype(jnp.bfloat16)
    return jnp.zeros_like(rounded).at[:, :, new_slot, :].set(rounded)
```

```python
import functools

import jax
import jax.numpy as jnp
from jax import lax
from jax.experimental import pallas as pl
from jax.experimental.pallas import tpu as pltpu
from jax.sharding import PartitionSpec as P

STEPS = 2
MESH = pl.DeviceIdType.MESH
coupling = 1.5

vectors = (
    (1, 0, 0), (1, 1, 0), (1, -1, 0), (1, 0, 1), (1, 0, -1),
    (-1, 0, 0), (-1, 1, 0), (-1, -1, 0), (-1, 0, 1), (-1, 0, -1),
    (0, 1, 0), (0, -1, 0), (0, 0, 1), (0, 0, -1),
    (0, 1, 1), (0, 1, -1), (0, -1, 1), (0, -1, -1),
    (0, 0, 0),
)
x_lists = tuple(
    ((0, s, 0), (1, s, 0), (-1, s, 0), (0, s, 1), (0, s, -1)) for s in (1, -1)
)
y_lists = tuple(
    ((0, 0, s), (1, 0, s), (-1, 0, s), (0, 1, s), (0, -1, s)) for s in (1, -1)
)
pair_list = ((0, 0), (1, 1), (2, 2), (0, 1), (0, 2), (1, 2))
PAD = 8


def kernel(
    sizes, phase, velocity, stress, sorting, info, out,
    moments, psi, psi_xs, psi_xr, psi_xyr, psi_ys, psi_yr, psi_zy, psi_rows,
    field_a, field_dx, field_dy, field_gx, field_gy,
    pops, pop_xs, pop_xr, pop_xyr, pop_ys, pop_yr, pop_zy,
    sent, arrived, info_in,
    send_sem, recv_sem, move_send, move_recv, info_send, info_recv,
):
    normal, planes, group_z, depth, width, breadth = sizes
    groups = depth // group_z
    me_z = lax.axis_index("normal")
    me_x = lax.axis_index("plane")
    me_y = lax.axis_index("inner")

    def device(offset):
        place = {}
        if offset[0] % normal:
            place["normal"] = lax.rem(me_z + offset[0] % normal, normal)
        if offset[1] % planes:
            place["plane"] = lax.rem(me_x + offset[1] % planes, planes)
        if offset[2] % 2:
            place["inner"] = 1 - me_y
        return place

    around = [
        (0, 0, 1), (1, 0, 0), (-1, 0, 0), (0, 1, 0), (0, -1, 0),
        (1, 0, 1), (-1, 0, 1), (0, 1, 1), (0, -1, 1),
        (1, 1, 0), (-1, 1, 0), (1, -1, 0), (-1, -1, 0),
    ]
    partners = sorted(
        {(a % normal, b % planes, c % 2) for a, b, c in around}
        | {(0, k, 0) for k in range(1, planes)}
    )
    barrier = pltpu.get_barrier_semaphore()
    for offset in partners:
        pl.semaphore_signal(barrier, inc=1, device_id=device(offset), device_id_type=MESH)

    lane = lax.broadcasted_iota(jnp.int32, (width, breadth), 1)
    row = lax.broadcasted_iota(jnp.int32, (width, breadth), 0)
    last = breadth - 1

    def start(kind, step, pairs):
        copies = []
        for number, (offset, (source, target)) in enumerate(zip(around, pairs)):
            copy = pltpu.make_async_remote_copy(
                src_ref=source,
                dst_ref=target,
                send_sem=send_sem.at[kind, step, number],
                recv_sem=recv_sem.at[kind, step, number],
                device_id=device(offset),
                device_id_type=MESH,
            )
            copy.start()
            copies.append(copy)
        return copies

    def from_low_x(value, edge):
        return jnp.where(row == 0, edge, pltpu.roll(value, 1, 0))

    def from_high_x(value, edge):
        return jnp.where(row == width - 1, edge, pltpu.roll(value, width - 1, 0))

    def initial(z, carry):
        density = jnp.where(phase[z] == 1, 2.0, 0.3).astype(jnp.float32)
        speed = [velocity[a, z] for a in range(3)]
        momentum = [density * s for s in speed]
        third = density * (1.0 / 3.0)
        moments[0, z] = density
        for a in range(3):
            moments[1 + a, z] = momentum[a]
        for k, (a, b) in enumerate(pair_list):
            second = momentum[a] * speed[b] + stress[k, z]
            moments[4 + k, z] = second + third if a == b else second
        return carry

    lax.fori_loop(0, depth, initial, 0)
    pl.semaphore_wait(barrier, len(partners))

    info_copies = []
    for k in range(1, planes):
        copy = pltpu.make_async_remote_copy(
            src_ref=info.at[lax.rem(me_x + k, planes)],
            dst_ref=info_in.at[k],
            send_sem=info_send.at[k],
            recv_sem=info_recv.at[k],
            device_id=device((0, k, 0)),
            device_id_type=MESH,
        )
        copy.start()
        info_copies.append(copy)

    def one_step(step, carry):
        def potential(z, packed):
            value = 1.0 - jnp.exp(-moments[0, z])
            psi[step, z + 1] = value
            psi_xs[step, 0, pl.ds(z, 1), :] = value[width - 1 : width]
            psi_xs[step, 1, pl.ds(z, 1), :] = value[0:1]
            packed = jnp.where(lane == z + 17, pltpu.roll(value, z + 18, 1), packed)
            return jnp.where(lane == z + 65, pltpu.roll(value, z + 65, 1), packed)

        psi_ys[step] = lax.fori_loop(
            0, depth, potential, jnp.zeros((width, breadth), jnp.float32)
        )
        low, high = pl.ds(0, PAD), pl.ds(depth - PAD, PAD)
        inner_rows = pl.ds(PAD, depth)
        before, after = pl.ds(0, PAD), pl.ds(depth + PAD, PAD)
        copies = start(0, step, [
            (psi_ys.at[step], psi_yr.at[step]),
            (psi.at[step, depth], psi.at[step, 0]),
            (psi.at[step, 1], psi.at[step, depth + 1]),
            (psi_xs.at[step, 0], psi_xr.at[step, 0, inner_rows]),
            (psi_xs.at[step, 1], psi_xr.at[step, 1, inner_rows]),
            (psi.at[step, depth], psi_zy.at[step, 0]),
            (psi.at[step, 1], psi_zy.at[step, 1]),
            (psi_xs.at[step, 0], psi_xyr.at[step, 0, inner_rows]),
            (psi_xs.at[step, 1], psi_xyr.at[step, 1, inner_rows]),
            (psi_xs.at[step, 0, high], psi_xr.at[step, 0, before]),
            (psi_xs.at[step, 0, low], psi_xr.at[step, 0, after]),
            (psi_xs.at[step, 1, high], psi_xr.at[step, 1, before]),
            (psi_xs.at[step, 1, low], psi_xr.at[step, 1, after]),
        ])
        for copy in copies:
            copy.wait()
        columns = psi_yr[step]
        for side, z_at in ((0, 16), (1, 17 + depth)):
            plane_in = psi_zy[step, side]
            columns = jnp.where(lane == z_at, pltpu.roll(plane_in, z_at + 1, 1), columns)
            columns = jnp.where(lane == z_at + 48, pltpu.roll(plane_in, z_at + 48, 1), columns)
        psi_yr[step] = columns
        rows_lane = lax.broadcasted_iota(jnp.int32, (depth + 2 * PAD, breadth), 1)
        for side in range(2):
            own, other = psi_xr[step, side], psi_xyr[step, side]
            psi_rows[0, side] = pltpu.roll(jnp.where(rows_lane == last, other, own), 1, 1)
            psi_rows[1, side] = pltpu.roll(jnp.where(rows_lane == 0, other, own), last, 1)

        def differences(p, carry):
            value = psi[step, p]
            columns = psi_yr[step]
            at = pl.ds(p + PAD - 1, 1)
            y_low = jnp.where(
                lane == 0, pltpu.roll(columns, 112 - p, 1), pltpu.roll(value, 1, 1)
            )
            y_high = jnp.where(
                lane == last, pltpu.roll(columns, 63 - p, 1), pltpu.roll(value, last, 1)
            )
            y_sum, y_diff = y_high + y_low, y_high - y_low
            x_low = from_low_x(value, psi_xr[step, 0, at, :])
            x_high = from_high_x(value, psi_xr[step, 1, at, :])
            edges = [
                [psi_rows[s, side, at, :] for s in range(2)] for side in range(2)
            ]
            x_diff = x_high - x_low
            field_a[p] = 2.0 * value + (x_high + x_low) + y_sum
            field_dx[p] = x_diff
            field_dy[p] = y_diff
            field_gx[p] = (
                2.0 * x_diff
                + from_high_x(y_sum, edges[1][1] + edges[1][0])
                - from_low_x(y_sum, edges[0][1] + edges[0][0])
            )
            field_gy[p] = (
                2.0 * y_diff
                + from_high_x(y_diff, edges[1][1] - edges[1][0])
                + from_low_x(y_diff, edges[0][1] - edges[0][0])
            )
            return carry

        lax.fori_loop(0, depth + 2, differences, 0)

        def collide(z, packs):
            p = z + 1
            scale = (coupling / 36.0) * psi[step, p]
            force = [
                scale * (field_a[p + 1] - field_a[p - 1]),
                scale * (field_gx[p] + (field_dx[p + 1] + field_dx[p - 1])),
                scale * (field_gy[p] + (field_dy[p + 1] + field_dy[p - 1])),
            ]
            density = moments[0, z]
            inverse = 1.0 / density
            momentum = [moments[1 + a, z] for a in range(3)]
            speed = [m * inverse for m in momentum]
            post = [m + f for m, f in zip(momentum, force)]
            second = {}
            for k, (a, b) in enumerate(pair_list):
                value = (
                    0.625 * (momentum[a] * speed[b])
                    + 0.375 * moments[4 + k, z]
                    + (speed[a] * force[b] + force[a] * speed[b])
                )
                if a == b:
                    second[a, a] = (value - 0.125 * density) * 0.125
                else:
                    second[a, b] = value * 0.25
            flow = [m * (1.0 / 12.0) for m in post]
            base = density * (1.0 / 36.0) - (
                second[0, 0] + second[1, 1] + second[2, 2]
            ) * (1.0 / 3.0)
            value_of = {(0, 0, 0): 12.0 * base}
            for a in range(3):
                even = 2.0 * (base + second[a, a])
                odd = 2.0 * flow[a]
                for sign in (1, -1):
                    vector = [0, 0, 0]
                    vector[a] = sign
                    value_of[tuple(vector)] = even + odd if sign == 1 else even - odd
            for a, b in pair_list[3:]:
                both = base + (second[a, a] + second[b, b])
                for sign in (1, -1):
                    if sign == 1:
                        even, odd = both + second[a, b], flow[a] + flow[b]
                    else:
                        even, odd = both - second[a, b], flow[a] - flow[b]
                    vector = [0, 0, 0]
                    vector[a], vector[b] = 1, sign
                    value_of[tuple(vector)] = even + odd
                    vector[a], vector[b] = -1, -sign
                    value_of[tuple(vector)] = even - odd
            for index, vector in enumerate(vectors):
                pops[step, index, p] = value_of[vector]
            for k in range(5):
                pop_xs[step, 0, k, pl.ds(z, 1), :] = value_of[x_lists[0][k]][width - 1 : width]
                pop_xs[step, 1, k, pl.ds(z, 1), :] = value_of[x_lists[1][k]][0:1]
            up, down = packs
            for k in range(5):
                at = p + 18 * k
                up = jnp.where(lane == at, pltpu.roll(value_of[y_lists[0][k]], at + 1, 1), up)
                down = jnp.where(lane == at, pltpu.roll(value_of[y_lists[1][k]], at, 1), down)
            return up, down

        nothing = jnp.zeros((width, breadth), jnp.float32)
        up, down = lax.fori_loop(0, depth, collide, (nothing, nothing))
        pop_ys[step, 0] = up
        pop_ys[step, 1] = down
        five, two = pl.ds(0, 5), pl.ds(3, 2)
        copies = start(1, step, [
            (pop_ys.at[step], pop_yr.at[step]),
            (pops.at[step, five, depth], pops.at[step, five, 0]),
            (pops.at[step, pl.ds(5, 5), 1], pops.at[step, pl.ds(5, 5), depth + 1]),
            (pop_xs.at[step, 0], pop_xr.at[step, 0, five, inner_rows]),
            (pop_xs.at[step, 1], pop_xr.at[step, 1, five, inner_rows]),
            (pops.at[step, two, depth], pop_zy.at[step, 0]),
            (pops.at[step, pl.ds(8, 2), 1], pop_zy.at[step, 1]),
            (pop_xs.at[step, 0, two], pop_xyr.at[step, 0]),
            (pop_xs.at[step, 1, two], pop_xyr.at[step, 1]),
            (pop_xs.at[step, 0, 1, high], pop_xr.at[step, 0, 1, before]),
            (pop_xs.at[step, 0, 2, low], pop_xr.at[step, 0, 2, after]),
            (pop_xs.at[step, 1, 1, high], pop_xr.at[step, 1, 1, before]),
            (pop_xs.at[step, 1, 2, low], pop_xr.at[step, 1, 2, after]),
        ])
        for copy in copies:
            copy.wait()
        for side in range(2):
            own = pop_xr[step, side, 3, inner_rows, :]
            other = pop_xyr[step, side, 0]
            pop_xr[step, side, 3, inner_rows, :] = pltpu.roll(
                jnp.where(lane == last, other, own), 1, 1
            )
            own = pop_xr[step, side, 4, inner_rows, :]
            other = pop_xyr[step, side, 1]
            pop_xr[step, side, 4, inner_rows, :] = pltpu.roll(
                jnp.where(lane == 0, other, own), last, 1
            )
        far = 36 + depth + 1
        up, down = pop_yr[step, 0], pop_yr[step, 1]
        up = jnp.where(lane == 18, pltpu.roll(pop_zy[step, 0, 0], 19, 1), up)
        down = jnp.where(lane == 18, pltpu.roll(pop_zy[step, 0, 1], 18, 1), down)
        up = jnp.where(lane == far, pltpu.roll(pop_zy[step, 1, 0], far + 1, 1), up)
        down = jnp.where(lane == far, pltpu.roll(pop_zy[step, 1, 1], far, 1), down)
        pop_yr[step, 0] = up
        pop_yr[step, 1] = down

        def stream(z, carry):
            up, down = pop_yr[step, 0], pop_yr[step, 1]
            passed = {}
            for index, vector in enumerate(vectors):
                p = z + 1 - vector[0]
                value = pops[step, index, p]
                if vector[2] == 1:
                    at = p + 18 * y_lists[0].index(vector)
                    value = jnp.where(
                        lane == 0, pltpu.roll(up, 128 - at, 1), pltpu.roll(value, 1, 1)
                    )
                elif vector[2] == -1:
                    at = p + 18 * y_lists[1].index(vector)
                    value = jnp.where(
                        lane == last, pltpu.roll(down, 127 - at, 1), pltpu.roll(value, last, 1)
                    )
                if vector[1] == 1:
                    k = x_lists[0].index(vector)
                    value = from_low_x(value, pop_xr[step, 0, k, pl.ds(p + PAD - 1, 1), :])
                elif vector[1] == -1:
                    k = x_lists[1].index(vector)
                    value = from_high_x(value, pop_xr[step, 1, k, pl.ds(p + PAD - 1, 1), :])
                passed[vector] = value
            totals, moved = {}, {}
            for a in range(3):
                vector = [0, 0, 0]
                vector[a] = 1
                plus = passed[tuple(vector)]
                vector[a] = -1
                minus = passed[tuple(vector)]
                totals[a], moved[a] = plus + minus, plus - minus
            axis_sum = totals[0] + totals[1] + totals[2]
            cross, pair_sum = {}, {}
            for a, b in pair_list[3:]:
                found = {}
                for sign_a in (1, -1):
                    for sign_b in (1, -1):
                        vector = [0, 0, 0]
                        vector[a], vector[b] = sign_a, sign_b
                        found[sign_a, sign_b] = passed[tuple(vector)]
                same = found[1, 1] + found[-1, -1]
                mixed = found[1, -1] + found[-1, 1]
                same_odd = found[1, 1] - found[-1, -1]
                mixed_odd = found[1, -1] - found[-1, 1]
                cross[a, b] = same - mixed
                pair_sum[a, b] = same + mixed
                moved[a] = moved[a] + (same_odd + mixed_odd)
                moved[b] = moved[b] + (same_odd - mixed_odd)
            moments[0, z] = passed[0, 0, 0] + axis_sum + (
                pair_sum[0, 1] + pair_sum[0, 2] + pair_sum[1, 2]
            )
            for a in range(3):
                moments[1 + a, z] = moved[a]
            moments[4, z] = totals[0] + (pair_sum[0, 1] + pair_sum[0, 2])
            moments[5, z] = totals[1] + (pair_sum[0, 1] + pair_sum[1, 2])
            moments[6, z] = totals[2] + (pair_sum[0, 2] + pair_sum[1, 2])
            for k, pair in enumerate(pair_list[3:]):
                moments[7 + k, z] = cross[pair]
            return carry

        lax.fori_loop(0, depth, stream, 0)
        return carry

    lax.fori_loop(0, STEPS, one_step, 0)

    order = sorting[...]
    tile = order.shape[0] // planes
    moves = []
    for g in range(groups):
        def arrange(c, carry):
            block = moments[c, pl.ds(g * group_z, group_z)].reshape(group_z * width, breadth)
            rows = jnp.dot(
                order, block.astype(jnp.bfloat16), preferred_element_type=jnp.float32
            ).astype(jnp.bfloat16)
            sent[g, :, c] = rows.reshape(planes, tile, breadth)
            return carry

        lax.fori_loop(0, 10, arrange, 0)
        for k in range(planes - 1, 0, -1):
            copy = pltpu.make_async_remote_copy(
                src_ref=sent.at[g, lax.rem(me_x + k, planes)],
                dst_ref=arrived.at[g, k],
                send_sem=move_send.at[g, k],
                recv_sem=move_recv.at[g, k],
                device_id=device((0, k, 0)),
                device_id_type=MESH,
            )
            copy.start()
            moves.append((g, copy))
        arrived[g, 0] = sent[g, me_x]

    for copy in info_copies:
        copy.wait()
    slots = planes * tile
    parts = [info[me_x, 0:1, 0:tile]]
    for k in range(1, planes):
        parts.append(info_in[k, 0:1, 0:tile])
    place = jnp.concatenate(parts, axis=1)
    to_row = lax.broadcasted_iota(jnp.int32, (group_z * width, slots), 0)
    from_slot = lax.broadcasted_iota(jnp.int32, (group_z * width, slots), 1)
    capacity = tile // group_z
    fits = (place == lax.rem(to_row, width).astype(jnp.float32)) & (
        lax.rem(from_slot, tile) // capacity == to_row // width
    )
    placing = jnp.where(fits, 1.0, 0.0).astype(jnp.bfloat16)
    for g in range(groups):
        for held, copy in moves:
            if held == g:
                copy.wait()

        def put(c, carry):
            rows = jnp.dot(
                placing,
                arrived[g, :, c].reshape(slots, breadth),
                preferred_element_type=jnp.float32,
            ).astype(jnp.bfloat16)
            out[c, pl.ds(g * group_z, group_z)] = rows.reshape(group_z, width, breadth)
            return carry

        lax.fori_loop(0, 10, put, 0)


def shards(mesh_sizes, phase, velocity, stress, new_slot):
    normal, planes = mesh_sizes
    depth, width, breadth = phase.shape
    capacity = 2 * ((width // 2 + planes - 1) // planes)
    group_z = 16 // capacity
    target = new_slot // width
    position = new_slot % width
    matches = (target[:, None] == jnp.arange(planes, dtype=jnp.int32)[None, :]).astype(jnp.int32)
    earlier = jnp.cumsum(matches, axis=0) - matches
    order_in = jnp.sum(earlier * matches, axis=1)
    slot_index = target * capacity + order_in
    chosen = slot_index[None, :] == jnp.arange(planes * capacity, dtype=jnp.int32)[:, None]
    place = jnp.sum(jnp.where(chosen, position[None, :] + 1, 0), axis=1) - 1
    same = jnp.arange(group_z)[:, None] == jnp.arange(group_z)[None, :]
    sorting = (
        chosen.reshape(planes, 1, capacity, 1, width) & same[None, :, None, :, None]
    ).reshape(planes * 16, group_z * width).astype(jnp.bfloat16)
    info = jnp.tile(place.reshape(planes, 1, capacity), (1, group_z, 1)).reshape(planes, 1, 16)
    info = jnp.pad(
        jnp.broadcast_to(info, (planes, 8, 16)).astype(jnp.float32),
        ((0, 0), (0, 0), (0, 112)),
    )
    groups = depth // group_z
    plane = (width, breadth)
    padded = (depth + 2 * PAD, breadth)
    f32, bf16 = jnp.float32, jnp.bfloat16
    vmem = pltpu.VMEM
    dma = pltpu.SemaphoreType.DMA
    whole = pl.BlockSpec(memory_space=pltpu.VMEM)
    return pl.pallas_call(
        functools.partial(kernel, (normal, planes, group_z, depth, width, breadth)),
        out_shape=jax.ShapeDtypeStruct((10, depth, width, breadth), bf16),
        in_specs=[whole] * 5,
        out_specs=whole,
        scratch_shapes=[
            vmem((10, depth) + plane, f32),
            vmem((STEPS, depth + 2) + plane, f32),
            vmem((STEPS, 2, depth, breadth), f32),
            vmem((STEPS, 2) + padded, f32),
            vmem((STEPS, 2) + padded, f32),
            vmem((STEPS,) + plane, f32),
            vmem((STEPS,) + plane, f32),
            vmem((STEPS, 2) + plane, f32),
            vmem((2, 2) + padded, f32),
        ]
        + [vmem((depth + 2,) + plane, f32)] * 5
        + [
            vmem((STEPS, 19, depth + 2) + plane, f32),
            vmem((STEPS, 2, 5, depth, breadth), f32),
            vmem((STEPS, 2, 5) + padded, f32),
            vmem((STEPS, 2, 2, depth, breadth), f32),
            vmem((STEPS, 2) + plane, f32),
            vmem((STEPS, 2) + plane, f32),
            vmem((STEPS, 2, 2) + plane, f32),
            vmem((groups, planes, 10, 16, breadth), bf16),
            vmem((groups, planes, 10, 16, breadth), bf16),
            vmem((planes, 8, 128), f32),
            dma((2, STEPS, 13)),
            dma((2, STEPS, 13)),
            dma((groups, planes)),
            dma((groups, planes)),
            dma((planes,)),
            dma((planes,)),
        ],
        compiler_params=pltpu.CompilerParams(
            collective_id=0, has_side_effects=True, vmem_limit_bytes=40 * 1024 * 1024
        ),
    )(phase, velocity, stress, sorting, info)


def solution(mesh):
    placed = (
        P(("groups", "normal"), "plane", "inner"),
        P(None, ("groups", "normal"), "plane", "inner"),
        P(None, ("groups", "normal"), "plane", "inner"),
        P(("groups", "plane")),
    )
    return jax.shard_map(
        functools.partial(shards, (mesh.shape["normal"], mesh.shape["plane"])),
        mesh=mesh,
        in_specs=placed,
        out_specs=P(None, ("groups", "normal"), "plane", "inner"),
        check_vma=False,
    )
```

```python
import functools

import jax
import jax.numpy as jnp
from jax import lax
from jax.experimental import pallas as pl
from jax.experimental.pallas import tpu as pltpu
from jax.sharding import PartitionSpec as P

STEPS = 2
MESH = pl.DeviceIdType.MESH
coupling = 1.5

vectors = (
    (1, 0, 0), (1, 1, 0), (1, -1, 0), (1, 0, 1), (1, 0, -1),
    (-1, 0, 0), (-1, 1, 0), (-1, -1, 0), (-1, 0, 1), (-1, 0, -1),
    (0, 1, 0), (0, -1, 0), (0, 0, 1), (0, 0, -1),
    (0, 1, 1), (0, 1, -1), (0, -1, 1), (0, -1, -1),
    (0, 0, 0),
)
x_lists = tuple(
    ((0, s, 0), (1, s, 0), (-1, s, 0), (0, s, 1), (0, s, -1)) for s in (1, -1)
)
y_lists = tuple(
    ((0, 0, s), (1, 0, s), (-1, 0, s), (0, 1, s), (0, -1, s)) for s in (1, -1)
)
pair_list = ((0, 0), (1, 1), (2, 2), (0, 1), (0, 2), (1, 2))
PAD = 8


def kernel(
    sizes, phase_hbm, velocity_hbm, stress_hbm, new_slot, out,
    phase, velocity, stress, moments, speeds, psi, psi_xs, psi_xr, psi_xyr, psi_ys, psi_yr, psi_zy, psi_rows,
    field_a, field_dx, field_dy, field_gx, field_gy,
    pops, pop_rows, pop_xs, pop_xin, pop_xyr, pop_zxr, pop_ys, pop_yr,
    pop_zs, pop_zin, pop_zy, side_sums, sent, arrived, info, info_in,
    load_sem, send_sem, recv_sem, move_send, move_recv, info_send, info_recv,
):
    normal, planes, group_z, depth, width, breadth = sizes
    groups = depth // group_z
    me_z = lax.axis_index("normal")
    me_x = lax.axis_index("plane")
    me_y = lax.axis_index("inner")

    def device(offset):
        place = {}
        if offset[0] % normal:
            place["normal"] = lax.rem(me_z + offset[0] % normal, normal)
        if offset[1] % planes:
            place["plane"] = lax.rem(me_x + offset[1] % planes, planes)
        if offset[2] % 2:
            place["inner"] = 1 - me_y
        return place

    around = [
        (0, 0, 1), (1, 0, 0), (-1, 0, 0), (0, 1, 0), (0, -1, 0),
        (1, 0, 1), (-1, 0, 1), (0, 1, 1), (0, -1, 1),
        (1, 1, 0), (-1, 1, 0), (1, -1, 0), (-1, -1, 0),
    ]
    partners = sorted(
        {(a % normal, b % planes, c % 2) for a, b, c in around}
        | {(0, k, 0) for k in range(1, planes)}
    )
    loads = [
        pltpu.make_async_copy(source, target, load_sem.at[number])
        for number, (source, target) in enumerate(
            ((phase_hbm, phase), (velocity_hbm, velocity), (stress_hbm, stress))
        )
    ]
    for load in loads:
        load.start()
    barrier = pltpu.get_barrier_semaphore()
    for offset in partners:
        pl.semaphore_signal(barrier, inc=1, device_id=device(offset), device_id_type=MESH)

    lane = lax.broadcasted_iota(jnp.int32, (width, breadth), 1)
    row = lax.broadcasted_iota(jnp.int32, (width, breadth), 0)
    last = breadth - 1

    def start(kind, step, pairs):
        copies = []
        for number, (offset, (source, target)) in enumerate(zip(around, pairs)):
            copy = pltpu.make_async_remote_copy(
                src_ref=source,
                dst_ref=target,
                send_sem=send_sem.at[kind, step, number],
                recv_sem=recv_sem.at[kind, step, number],
                device_id=device(offset),
                device_id_type=MESH,
            )
            copy.start()
            copies.append(copy)
        return copies

    def from_low_x(value, edge):
        return jnp.where(row == 0, edge, pltpu.roll(value, 1, 0))

    def from_high_x(value, edge):
        return jnp.where(row == width - 1, edge, pltpu.roll(value, width - 1, 0))

    def initial(z, carry):
        density = moments[0, z]
        speed = [velocity[a, z] for a in range(3)]
        momentum = [density * s for s in speed]
        for a in range(3):
            moments[1 + a, z] = momentum[a]
            speeds[a, z] = speed[a]
        for k, (a, b) in enumerate(pair_list):
            moments[4 + k, z] = momentum[a] * speed[b] + 0.375 * stress[k, z]
        return carry

    def prepare(z, carry):
        density = moments[0, z]
        inverse = 1.0 / density
        momentum = [moments[1 + a, z] for a in range(3)]
        speed = [m * inverse for m in momentum]
        eighth = 0.125 * density
        for a in range(3):
            speeds[a, z] = speed[a]
        for k, (a, b) in enumerate(pair_list):
            value = 0.625 * (momentum[a] * speed[b]) + 0.375 * moments[4 + k, z]
            moments[4 + k, z] = value - eighth if a == b else value
        return carry

    def start_density(z, carry):
        moments[0, z] = jnp.where(phase[z] == 1, 2.0, 0.3).astype(jnp.float32)
        return carry

    loads[0].wait()
    lax.fori_loop(0, depth, start_density, 0, unroll=4)

    tile = 16
    capacity = tile // group_z
    info_copies = []

    def plan():
        slots = planes * tile
        blocks = [new_slot[x] for x in range(width)]
        owners = [lax.div(block, width) for block in blocks]
        places = [lax.rem(block, width) for block in blocks]
        at_slot = []
        for x in range(width):
            earlier = jnp.int32(0)
            for other in range(x):
                earlier = earlier + jnp.where(owners[other] == owners[x], 1, 0)
            at_slot.append(owners[x] * capacity + earlier)
        shape = (slots, group_z * width)
        to_slot = lax.broadcasted_iota(jnp.int32, shape, 0)
        from_cell = lax.broadcasted_iota(jnp.int32, shape, 1)
        from_x = lax.rem(from_cell[0:8], width)
        slot_of = jnp.zeros(from_x.shape, jnp.int32)
        for x in range(width):
            slot_of = jnp.where(from_x == x, at_slot[x], slot_of)
        here = lax.div(to_slot, tile) * capacity + lax.rem(to_slot, capacity)
        layer = lax.div(lax.rem(to_slot, tile), capacity)
        chosen = (slot_of[0:1] == here) & (layer == lax.div(from_cell, width))
        order = jnp.where(chosen, 1.0, 0.0).astype(jnp.bfloat16)
        small = lax.broadcasted_iota(jnp.int32, (8, 128), 1)
        for t in range(planes):
            wanted = lax.rem(small, capacity) + t * capacity
            place = jnp.full((8, 128), -1, jnp.int32)
            for x in range(width):
                place = jnp.where(wanted == at_slot[x], places[x], place)
            info[t] = place.astype(jnp.float32)
        for k in range(1, planes):
            copy = pltpu.make_async_remote_copy(
                src_ref=info.at[lax.rem(me_x + k, planes)],
                dst_ref=info_in.at[k],
                send_sem=info_send.at[k],
                recv_sem=info_recv.at[k],
                device_id=device((0, k, 0)),
                device_id_type=MESH,
            )
            copy.start()
            info_copies.append(copy)
        return order

    for step in range(STEPS):
        def potential(z, packed):
            value = 1.0 - jnp.exp(-moments[0, z])
            psi[step, z + 1] = value
            psi_xs[step, 0, pl.ds(z, 1), :] = value[width - 1 : width]
            psi_xs[step, 1, pl.ds(z, 1), :] = value[0:1]
            packed = jnp.where(lane == z + 17, pltpu.roll(value, z + 18, 1), packed)
            return jnp.where(lane == z + 65, pltpu.roll(value, z + 65, 1), packed)

        psi_ys[step] = lax.fori_loop(
            0, depth, potential, jnp.zeros((width, breadth), jnp.float32), unroll=4
        )
        low, high = pl.ds(0, PAD), pl.ds(depth - PAD, PAD)
        inner_rows = pl.ds(PAD, depth)
        before, after = pl.ds(0, PAD), pl.ds(depth + PAD, PAD)
        if step == 0:
            pl.semaphore_wait(barrier, len(partners))
        copies = start(0, step, [
            (psi_ys.at[step], psi_yr.at[step]),
            (psi.at[step, depth], psi.at[step, 0]),
            (psi.at[step, 1], psi.at[step, depth + 1]),
            (psi_xs.at[step, 0], psi_xr.at[step, 0, inner_rows]),
            (psi_xs.at[step, 1], psi_xr.at[step, 1, inner_rows]),
            (psi.at[step, depth], psi_zy.at[step, 0]),
            (psi.at[step, 1], psi_zy.at[step, 1]),
            (psi_xs.at[step, 0], psi_xyr.at[step, 0, inner_rows]),
            (psi_xs.at[step, 1], psi_xyr.at[step, 1, inner_rows]),
            (psi_xs.at[step, 0, high], psi_xr.at[step, 0, before]),
            (psi_xs.at[step, 0, low], psi_xr.at[step, 0, after]),
            (psi_xs.at[step, 1, high], psi_xr.at[step, 1, before]),
            (psi_xs.at[step, 1, low], psi_xr.at[step, 1, after]),
        ])
        if step == 0:
            order = plan()
            loads[1].wait()
            loads[2].wait()
            lax.fori_loop(0, depth, initial, 0)
        else:
            lax.fori_loop(0, depth, prepare, 0)
        for copy in copies:
            copy.wait()
        columns = psi_yr[step]
        for side, z_at in ((0, 16), (1, 17 + depth)):
            plane_in = psi_zy[step, side]
            columns = jnp.where(lane == z_at, pltpu.roll(plane_in, z_at + 1, 1), columns)
            columns = jnp.where(lane == z_at + 48, pltpu.roll(plane_in, z_at + 48, 1), columns)
        psi_yr[step] = columns
        rows_lane = lax.broadcasted_iota(jnp.int32, (depth + 2 * PAD, breadth), 1)
        for side in range(2):
            own, other = psi_xr[step, side], psi_xyr[step, side]
            psi_rows[0, side] = pltpu.roll(jnp.where(rows_lane == last, other, own), 1, 1)
            psi_rows[1, side] = pltpu.roll(jnp.where(rows_lane == 0, other, own), last, 1)

        def differences(p, carry):
            value = psi[step, p]
            columns = psi_yr[step]
            at = pl.ds(p + PAD - 1, 1)
            y_low = jnp.where(
                lane == 0, pltpu.roll(columns, 112 - p, 1), pltpu.roll(value, 1, 1)
            )
            y_high = jnp.where(
                lane == last, pltpu.roll(columns, 63 - p, 1), pltpu.roll(value, last, 1)
            )
            y_sum, y_diff = y_high + y_low, y_high - y_low
            x_low = from_low_x(value, psi_xr[step, 0, at, :])
            x_high = from_high_x(value, psi_xr[step, 1, at, :])
            edges = [
                [psi_rows[s, side, at, :] for s in range(2)] for side in range(2)
            ]
            x_diff = x_high - x_low
            field_a[p] = 2.0 * value + (x_high + x_low) + y_sum
            field_dx[p] = x_diff
            field_dy[p] = y_diff
            field_gx[p] = (
                2.0 * x_diff
                + from_high_x(y_sum, edges[1][1] + edges[1][0])
                - from_low_x(y_sum, edges[0][1] + edges[0][0])
            )
            field_gy[p] = (
                2.0 * y_diff
                + from_high_x(y_diff, edges[1][1] - edges[1][0])
                + from_low_x(y_diff, edges[0][1] - edges[0][0])
            )
            return carry

        lax.fori_loop(0, depth + 2, differences, 0, unroll=2)

        def collide(z, packs):
            p = z + 1
            scale = (coupling / 36.0) * psi[step, p]
            force = [
                scale * (field_a[p + 1] - field_a[p - 1]),
                scale * (field_gx[p] + (field_dx[p + 1] + field_dx[p - 1])),
                scale * (field_gy[p] + (field_dy[p + 1] + field_dy[p - 1])),
            ]
            density = moments[0, z]
            momentum = [moments[1 + a, z] for a in range(3)]
            speed = [speeds[a, z] for a in range(3)]
            post = [m + f for m, f in zip(momentum, force)]
            second = {}
            for k, (a, b) in enumerate(pair_list):
                value = moments[4 + k, z] + (speed[a] * force[b] + force[a] * speed[b])
                second[a, b] = value * (0.125 if a == b else 0.25)
            flow = [m * (1.0 / 12.0) for m in post]
            base = density * (1.0 / 36.0) - (
                second[0, 0] + second[1, 1] + second[2, 2]
            ) * (1.0 / 3.0)
            value_of = {(0, 0, 0): 12.0 * base}
            for a in range(3):
                even = 2.0 * (base + second[a, a])
                odd = 2.0 * flow[a]
                for sign in (1, -1):
                    vector = [0, 0, 0]
                    vector[a] = sign
                    value_of[tuple(vector)] = even + odd if sign == 1 else even - odd
            for a, b in pair_list[3:]:
                both = base + (second[a, a] + second[b, b])
                for sign in (1, -1):
                    if sign == 1:
                        even, odd = both + second[a, b], flow[a] + flow[b]
                    else:
                        even, odd = both - second[a, b], flow[a] - flow[b]
                    vector = [0, 0, 0]
                    vector[a], vector[b] = 1, sign
                    value_of[tuple(vector)] = even + odd
                    vector[a], vector[b] = -1, -sign
                    value_of[tuple(vector)] = even - odd
            for index, vector in enumerate(vectors):
                pops[step, index, p] = value_of[vector]
            for k in range(5):
                pop_rows[0, k, pl.ds(z, 1), :] = value_of[x_lists[0][k]][width - 1 : width]
                pop_rows[1, k, pl.ds(z, 1), :] = value_of[x_lists[1][k]][0:1]
            up, down = packs
            for k in range(5):
                at = p + 18 * k
                up = jnp.where(lane == at, pltpu.roll(value_of[y_lists[0][k]], at + 1, 1), up)
                down = jnp.where(lane == at, pltpu.roll(value_of[y_lists[1][k]], at, 1), down)
            return up, down

        nothing = jnp.zeros((width, breadth), jnp.float32)
        up, down = lax.fori_loop(0, depth, collide, (nothing, nothing))
        pop_ys[step, 0] = up
        pop_ys[step, 1] = down
        for k in range(5):
            pop_zs[step, 0, k] = pops[step, k, depth].astype(jnp.bfloat16)
            pop_zs[step, 1, k] = pops[step, 5 + k, 1].astype(jnp.bfloat16)
            for side in range(2):
                pop_xs[step, side, k] = pop_rows[side, k].astype(jnp.bfloat16)
        two = pl.ds(3, 2)
        copies = start(1, step, [
            (pop_ys.at[step], pop_yr.at[step]),
            (pop_zs.at[step, 0], pop_zin.at[step, 0]),
            (pop_zs.at[step, 1], pop_zin.at[step, 1]),
            (pop_xs.at[step, 0], pop_xin.at[step, 0]),
            (pop_xs.at[step, 1], pop_xin.at[step, 1]),
            (pop_zs.at[step, 0, two], pop_zy.at[step, 0]),
            (pop_zs.at[step, 1, two], pop_zy.at[step, 1]),
            (pop_xs.at[step, 0, two], pop_xyr.at[step, 0]),
            (pop_xs.at[step, 1, two], pop_xyr.at[step, 1]),
            (pop_xs.at[step, 0, 1], pop_zxr.at[step, 0, 0]),
            (pop_xs.at[step, 0, 2], pop_zxr.at[step, 0, 1]),
            (pop_xs.at[step, 1, 1], pop_zxr.at[step, 1, 0]),
            (pop_xs.at[step, 1, 2], pop_zxr.at[step, 1, 1]),
        ])

        def stream(z, carry):
            up, down = pop_yr[step, 0], pop_yr[step, 1]
            passed = {}
            for index, vector in enumerate(vectors):
                p = z + 1 - vector[0]
                value = pops[step, index, p]
                if vector[2] == 1:
                    at = p + 18 * y_lists[0].index(vector)
                    value = jnp.where(
                        lane == 0, pltpu.roll(up, 128 - at, 1), pltpu.roll(value, 1, 1)
                    )
                elif vector[2] == -1:
                    at = p + 18 * y_lists[1].index(vector)
                    value = jnp.where(
                        lane == last, pltpu.roll(down, 127 - at, 1), pltpu.roll(value, last, 1)
                    )
                if vector[1] == 1:
                    value = from_low_x(value, 0.0)
                elif vector[1] == -1:
                    value = from_high_x(value, 0.0)
                passed[vector] = value
            totals, moved = {}, {}
            for a in range(3):
                vector = [0, 0, 0]
                vector[a] = 1
                plus = passed[tuple(vector)]
                vector[a] = -1
                minus = passed[tuple(vector)]
                totals[a], moved[a] = plus + minus, plus - minus
            axis_sum = totals[0] + totals[1] + totals[2]
            cross, pair_sum = {}, {}
            for a, b in pair_list[3:]:
                found = {}
                for sign_a in (1, -1):
                    for sign_b in (1, -1):
                        vector = [0, 0, 0]
                        vector[a], vector[b] = sign_a, sign_b
                        found[sign_a, sign_b] = passed[tuple(vector)]
                same = found[1, 1] + found[-1, -1]
                mixed = found[1, -1] + found[-1, 1]
                same_odd = found[1, 1] - found[-1, -1]
                mixed_odd = found[1, -1] - found[-1, 1]
                cross[a, b] = same - mixed
                pair_sum[a, b] = same + mixed
                moved[a] = moved[a] + (same_odd + mixed_odd)
                moved[b] = moved[b] + (same_odd - mixed_odd)
            moments[0, z] = passed[0, 0, 0] + axis_sum + (
                pair_sum[0, 1] + pair_sum[0, 2] + pair_sum[1, 2]
            )
            for a in range(3):
                moments[1 + a, z] = moved[a]
            moments[4, z] = totals[0] + (pair_sum[0, 1] + pair_sum[0, 2])
            moments[5, z] = totals[1] + (pair_sum[0, 1] + pair_sum[1, 2])
            moments[6, z] = totals[2] + (pair_sum[0, 2] + pair_sum[1, 2])
            for k, pair in enumerate(pair_list[3:]):
                moments[7 + k, z] = cross[pair]
            return carry

        copies[0].wait()
        lax.fori_loop(1, depth - 1, stream, 0)
        for copy in copies[1:]:
            copy.wait()
        f32 = jnp.float32
        for k in range(5):
            pops[step, k, 0] = pop_zin[step, 0, k].astype(f32)
            pops[step, 5 + k, depth + 1] = pop_zin[step, 1, k].astype(f32)
        far = 36 + depth + 1
        corner = [[pop_zy[step, side, k].astype(f32) for k in range(2)] for side in range(2)]
        up, down = pop_yr[step, 0], pop_yr[step, 1]
        up = jnp.where(lane == 18, pltpu.roll(corner[0][0], 19, 1), up)
        down = jnp.where(lane == 18, pltpu.roll(corner[0][1], 18, 1), down)
        up = jnp.where(lane == far, pltpu.roll(corner[1][0], far + 1, 1), up)
        down = jnp.where(lane == far, pltpu.roll(corner[1][1], far, 1), down)
        pop_yr[step, 0] = up
        pop_yr[step, 1] = down
        lax.fori_loop(0, 2, lambda i, carry: stream(i * (depth - 1), carry), 0)

        z_row = lax.broadcasted_iota(jnp.int32, (depth, breadth), 0)
        z_lane = lax.broadcasted_iota(jnp.int32, (depth, breadth), 1)
        for side in range(2):
            own = [pop_xin[step, side, k].astype(f32) for k in range(5)]
            edge = [pop_zxr[step, side, k].astype(f32) for k in range(2)]
            other = [pop_xyr[step, side, k].astype(f32) for k in range(2)]
            plain = own[0]
            z_up = jnp.where(z_row == 0, pltpu.roll(edge[0], 1, 0), pltpu.roll(own[1], 1, 0))
            z_down = jnp.where(
                z_row == depth - 1,
                pltpu.roll(edge[1], depth - 1, 0),
                pltpu.roll(own[2], depth - 1, 0),
            )
            y_up = pltpu.roll(jnp.where(z_lane == last, other[0], own[3]), 1, 1)
            y_down = pltpu.roll(jnp.where(z_lane == 0, other[1], own[4]), last, 1)
            z_even, z_odd = z_up + z_down, z_up - z_down
            y_even, y_odd = y_up + y_down, y_up - y_down
            total = plain + (z_even + y_even)
            if side == 0:
                adds = [total, z_odd, total, y_odd, z_even, total, y_even, z_odd, y_odd]
            else:
                adds = [total, z_odd, -total, y_odd, z_even, total, y_even, -z_odd, -y_odd]
            for k, add in enumerate(adds):
                side_sums[side, k] = add

        def add_sides(z, carry):
            at = pl.ds(z, 1)
            for k, c in enumerate((0, 1, 2, 3, 4, 5, 6, 7, 9)):
                for side, x in ((0, 0), (1, width - 1)):
                    cells = (c, z, pl.ds(x, 1), slice(None))
                    moments[cells] = moments[cells] + side_sums[side, k, at, :]
            return carry

        if step < STEPS - 1:
            lax.fori_loop(0, depth, add_sides, 0)

    moves = []
    for g in range(groups):
        lax.fori_loop(g * group_z, (g + 1) * group_z, add_sides, 0)
        block = jnp.concatenate(
            [
                moments[c, g * group_z : (g + 1) * group_z]
                .reshape(group_z * width, breadth)
                .astype(jnp.bfloat16)
                for c in range(10)
            ],
            axis=1,
        )
        rows = jnp.dot(order, block, preferred_element_type=jnp.float32).astype(jnp.bfloat16)
        for c in range(10):
            sent[g, :, c] = rows[:, c * breadth : (c + 1) * breadth].reshape(
                planes, tile, breadth
            )
        for k in range(planes - 1, 0, -1):
            copy = pltpu.make_async_remote_copy(
                src_ref=sent.at[g, lax.rem(me_x + k, planes)],
                dst_ref=arrived.at[g, k],
                send_sem=move_send.at[g, k],
                recv_sem=move_recv.at[g, k],
                device_id=device((0, k, 0)),
                device_id_type=MESH,
            )
            copy.start()
            moves.append((g, copy))
        arrived[g, 0] = sent[g, me_x]

    for copy in info_copies:
        copy.wait()
    slots = planes * tile
    parts = [info[me_x, 0:1, 0:tile]]
    for k in range(1, planes):
        parts.append(info_in[k, 0:1, 0:tile])
    place = jnp.concatenate(parts, axis=1)
    to_row = lax.broadcasted_iota(jnp.int32, (group_z * width, slots), 0)
    from_slot = lax.broadcasted_iota(jnp.int32, (group_z * width, slots), 1)
    fits = (place == lax.rem(to_row, width).astype(jnp.float32)) & (
        lax.rem(from_slot, tile) // capacity == to_row // width
    )
    placing = jnp.where(fits, 1.0, 0.0).astype(jnp.bfloat16)
    for g in range(groups):
        for held, copy in moves:
            if held == g:
                copy.wait()

        block = jnp.concatenate(
            [arrived[g, :, c].reshape(slots, breadth) for c in range(10)], axis=1
        )
        rows = jnp.dot(placing, block, preferred_element_type=jnp.float32).astype(jnp.bfloat16)
        for c in range(10):
            out[c, pl.ds(g * group_z, group_z)] = rows[
                :, c * breadth : (c + 1) * breadth
            ].reshape(group_z, width, breadth)


def shards(mesh_sizes, phase, velocity, stress, new_slot):
    normal, planes = mesh_sizes
    depth, width, breadth = phase.shape
    capacity = 2 * ((width // 2 + planes - 1) // planes)
    group_z = 16 // capacity
    groups = depth // group_z
    plane = (width, breadth)
    padded = (depth + 2 * PAD, breadth)
    f32, bf16 = jnp.float32, jnp.bfloat16
    vmem = pltpu.VMEM
    dma = pltpu.SemaphoreType.DMA
    whole = pl.BlockSpec(memory_space=pltpu.VMEM)
    return pl.pallas_call(
        functools.partial(kernel, (normal, planes, group_z, depth, width, breadth)),
        out_shape=jax.ShapeDtypeStruct((10, depth, width, breadth), bf16),
        in_specs=[pl.BlockSpec(memory_space=pltpu.HBM)] * 3
        + [pl.BlockSpec(memory_space=pltpu.SMEM)],
        out_specs=whole,
        scratch_shapes=[
            vmem((depth,) + plane, jnp.int32),
            vmem((3, depth) + plane, f32),
            vmem((6, depth) + plane, f32),
            vmem((10, depth) + plane, f32),
            vmem((3, depth) + plane, f32),
            vmem((STEPS, depth + 2) + plane, f32),
            vmem((STEPS, 2, depth, breadth), f32),
            vmem((STEPS, 2) + padded, f32),
            vmem((STEPS, 2) + padded, f32),
            vmem((STEPS,) + plane, f32),
            vmem((STEPS,) + plane, f32),
            vmem((STEPS, 2) + plane, f32),
            vmem((2, 2) + padded, f32),
        ]
        + [vmem((depth + 2,) + plane, f32)] * 5
        + [
            vmem((STEPS, 19, depth + 2) + plane, f32),
            vmem((2, 5, depth, breadth), f32),
            vmem((STEPS, 2, 5, depth, breadth), bf16),
            vmem((STEPS, 2, 5, depth, breadth), bf16),
            vmem((STEPS, 2, 2, depth, breadth), bf16),
            vmem((STEPS, 2, 2, depth, breadth), bf16),
            vmem((STEPS, 2) + plane, f32),
            vmem((STEPS, 2) + plane, f32),
            vmem((STEPS, 2, 5) + plane, bf16),
            vmem((STEPS, 2, 5) + plane, bf16),
            vmem((STEPS, 2, 2) + plane, bf16),
            vmem((2, 9, depth, breadth), f32),
            vmem((groups, planes, 10, 16, breadth), bf16),
            vmem((groups, planes, 10, 16, breadth), bf16),
            vmem((planes, 8, 128), f32),
            vmem((planes, 8, 128), f32),
            dma((3,)),
            dma((2, STEPS, 13)),
            dma((2, STEPS, 13)),
            dma((groups, planes)),
            dma((groups, planes)),
            dma((planes,)),
            dma((planes,)),
        ],
        compiler_params=pltpu.CompilerParams(
            collective_id=0, has_side_effects=True, vmem_limit_bytes=40 * 1024 * 1024
        ),
    )(phase, velocity, stress, new_slot)


def solution(mesh):
    placed = (
        P(("groups", "normal"), "plane", "inner"),
        P(None, ("groups", "normal"), "plane", "inner"),
        P(None, ("groups", "normal"), "plane", "inner"),
        P(("groups", "plane")),
    )
    return jax.shard_map(
        functools.partial(shards, (mesh.shape["normal"], mesh.shape["plane"])),
        mesh=mesh,
        in_specs=placed,
        out_specs=P(None, ("groups", "normal"), "plane", "inner"),
        check_vma=False,
    )
```

```python
import functools

import jax
import jax.numpy as jnp
from jax import lax
from jax.experimental import pallas as pl
from jax.experimental.pallas import tpu as pltpu
from jax.sharding import PartitionSpec as P

STEPS = 2
MESH = pl.DeviceIdType.MESH
coupling = 1.5

vectors = (
    (1, 0, 0), (1, 1, 0), (1, -1, 0), (1, 0, 1), (1, 0, -1),
    (-1, 0, 0), (-1, 1, 0), (-1, -1, 0), (-1, 0, 1), (-1, 0, -1),
    (0, 1, 0), (0, -1, 0), (0, 0, 1), (0, 0, -1),
    (0, 1, 1), (0, 1, -1), (0, -1, 1), (0, -1, -1),
    (0, 0, 0),
)
x_lists = tuple(
    ((0, s, 0), (1, s, 0), (-1, s, 0), (0, s, 1), (0, s, -1)) for s in (1, -1)
)
y_lists = tuple(
    ((0, 0, s), (1, 0, s), (-1, 0, s), (0, 1, s), (0, -1, s)) for s in (1, -1)
)
pair_list = ((0, 0), (1, 1), (2, 2), (0, 1), (0, 2), (1, 2))
PAD = 8


def kernel(
    sizes, phase_hbm, velocity_hbm, stress_hbm, new_slot, out,
    phase, velocity, stress, moments, speeds, psi, psi_xs, psi_xr, psi_xyr, psi_ys, psi_yr, psi_zy, psi_rows,
    field_a, field_dx, field_dy, field_gx, field_gy,
    pops, pop_rows, pop_xs, pop_xin, pop_xyr, pop_zxr, pop_ys, pop_yr,
    pop_zs, pop_zin, pop_zy, side_sums, sent, arrived, info, info_in,
    load_sem, send_sem, recv_sem, move_send, move_recv, info_send, info_recv,
):
    normal, planes, group_z, depth, width, breadth = sizes
    groups = depth // group_z
    me_z = lax.axis_index("normal")
    me_x = lax.axis_index("plane")
    me_y = lax.axis_index("inner")

    def device(offset):
        place = {}
        if offset[0] % normal:
            place["normal"] = lax.rem(me_z + offset[0] % normal, normal)
        if offset[1] % planes:
            place["plane"] = lax.rem(me_x + offset[1] % planes, planes)
        if offset[2] % 2:
            place["inner"] = 1 - me_y
        return place

    around = [
        (1, 1, 0), (-1, 1, 0), (1, -1, 0), (-1, -1, 0),
        (0, 1, 0), (0, -1, 0), (0, 1, 1), (0, -1, 1),
        (1, 0, 0), (-1, 0, 0), (1, 0, 1), (-1, 0, 1), (0, 0, 1),
    ]
    partners = []
    for a, b, c in around + [(0, k, 0) for k in range(1, planes)]:
        offset = (a % normal, b % planes, c % 2)
        if offset not in partners:
            partners.append(offset)
    loads = [
        pltpu.make_async_copy(source, target, load_sem.at[number])
        for number, (source, target) in enumerate(
            ((phase_hbm, phase), (velocity_hbm, velocity), (stress_hbm, stress))
        )
    ]
    for load in loads:
        load.start()
    barrier = pltpu.get_barrier_semaphore()
    for offset in partners:
        pl.semaphore_signal(barrier, inc=1, device_id=device(offset), device_id_type=MESH)

    lane = lax.broadcasted_iota(jnp.int32, (width, breadth), 1)
    row = lax.broadcasted_iota(jnp.int32, (width, breadth), 0)
    last = breadth - 1

    def start(kind, step, pairs):
        copies = []
        for number, (offset, (source, target)) in enumerate(zip(around, pairs)):
            copy = pltpu.make_async_remote_copy(
                src_ref=source,
                dst_ref=target,
                send_sem=send_sem.at[kind, step, number],
                recv_sem=recv_sem.at[kind, step, number],
                device_id=device(offset),
                device_id_type=MESH,
            )
            copy.start()
            copies.append(copy)
        return copies

    def from_low_x(value, edge):
        return jnp.where(row == 0, edge, pltpu.roll(value, 1, 0))

    def from_high_x(value, edge):
        return jnp.where(row == width - 1, edge, pltpu.roll(value, width - 1, 0))

    def initial(z, carry):
        density = moments[0, z]
        speed = [velocity[a, z] for a in range(3)]
        momentum = [density * s for s in speed]
        for a in range(3):
            moments[1 + a, z] = momentum[a]
            speeds[a, z] = speed[a]
        for k, (a, b) in enumerate(pair_list):
            moments[4 + k, z] = momentum[a] * speed[b] + 0.375 * stress[k, z]
        return carry

    def prepare(z, carry):
        density = moments[0, z]
        inverse = 1.0 / density
        momentum = [moments[1 + a, z] for a in range(3)]
        speed = [m * inverse for m in momentum]
        eighth = 0.125 * density
        for a in range(3):
            speeds[a, z] = speed[a]
        for k, (a, b) in enumerate(pair_list):
            value = 0.625 * (momentum[a] * speed[b]) + 0.375 * moments[4 + k, z]
            moments[4 + k, z] = value - eighth if a == b else value
        return carry

    def start_density(z, carry):
        moments[0, z] = jnp.where(phase[z] == 1, 2.0, 0.3).astype(jnp.float32)
        return carry

    loads[0].wait()
    lax.fori_loop(0, depth, start_density, 0, unroll=4)

    tile = 16
    capacity = tile // group_z
    info_copies = []

    def plan():
        slots = planes * tile
        blocks = [new_slot[x] for x in range(width)]
        owners = [lax.div(block, width) for block in blocks]
        places = [lax.rem(block, width) for block in blocks]
        at_slot = []
        for x in range(width):
            earlier = jnp.int32(0)
            for other in range(x):
                earlier = earlier + jnp.where(owners[other] == owners[x], 1, 0)
            at_slot.append(owners[x] * capacity + earlier)
        shape = (slots, group_z * width)
        to_slot = lax.broadcasted_iota(jnp.int32, shape, 0)
        from_cell = lax.broadcasted_iota(jnp.int32, shape, 1)
        from_x = lax.rem(from_cell[0:8], width)
        slot_of = jnp.zeros(from_x.shape, jnp.int32)
        for x in range(width):
            slot_of = jnp.where(from_x == x, at_slot[x], slot_of)
        here = lax.div(to_slot, tile) * capacity + lax.rem(to_slot, capacity)
        layer = lax.div(lax.rem(to_slot, tile), capacity)
        chosen = (slot_of[0:1] == here) & (layer == lax.div(from_cell, width))
        order = jnp.where(chosen, 1.0, 0.0).astype(jnp.bfloat16)
        small = lax.broadcasted_iota(jnp.int32, (8, 128), 1)
        for t in range(planes):
            wanted = lax.rem(small, capacity) + t * capacity
            place = jnp.full((8, 128), -1, jnp.int32)
            for x in range(width):
                place = jnp.where(wanted == at_slot[x], places[x], place)
            info[t] = place.astype(jnp.float32)
        return order

    def send_info():
        for k in range(1, planes):
            copy = pltpu.make_async_remote_copy(
                src_ref=info.at[lax.rem(me_x + k, planes)],
                dst_ref=info_in.at[k],
                send_sem=info_send.at[k],
                recv_sem=info_recv.at[k],
                device_id=device((0, k, 0)),
                device_id_type=MESH,
            )
            copy.start()
            info_copies.append(copy)

    order = plan()
    started = []
    for step in range(STEPS):
        def potential(z, packed):
            value = 1.0 - jnp.exp(-moments[0, z])
            psi[step, z + 1] = value
            psi_xs[step, 0, pl.ds(z, 1), :] = value[width - 1 : width]
            psi_xs[step, 1, pl.ds(z, 1), :] = value[0:1]
            packed = jnp.where(lane == z + 17, pltpu.roll(value, z + 18, 1), packed)
            return jnp.where(lane == z + 65, pltpu.roll(value, z + 65, 1), packed)

        psi_ys[step] = lax.fori_loop(
            0, depth, potential, jnp.zeros((width, breadth), jnp.float32), unroll=4
        )
        low, high = pl.ds(0, PAD), pl.ds(depth - PAD, PAD)
        inner_rows = pl.ds(PAD, depth)
        before, after = pl.ds(0, PAD), pl.ds(depth + PAD, PAD)
        if step == 0:
            pl.semaphore_wait(barrier, len(partners))
        copies = start(0, step, [
            (psi_xs.at[step, 0, high], psi_xr.at[step, 0, before]),
            (psi_xs.at[step, 0, low], psi_xr.at[step, 0, after]),
            (psi_xs.at[step, 1, high], psi_xr.at[step, 1, before]),
            (psi_xs.at[step, 1, low], psi_xr.at[step, 1, after]),
            (psi_xs.at[step, 0], psi_xr.at[step, 0, inner_rows]),
            (psi_xs.at[step, 1], psi_xr.at[step, 1, inner_rows]),
            (psi_xs.at[step, 0], psi_xyr.at[step, 0, inner_rows]),
            (psi_xs.at[step, 1], psi_xyr.at[step, 1, inner_rows]),
            (psi.at[step, depth], psi.at[step, 0]),
            (psi.at[step, 1], psi.at[step, depth + 1]),
            (psi.at[step, depth], psi_zy.at[step, 0]),
            (psi.at[step, 1], psi_zy.at[step, 1]),
            (psi_ys.at[step], psi_yr.at[step]),
        ])
        if step == 0:
            send_info()
            loads[1].wait()
            loads[2].wait()
            lax.fori_loop(0, depth, initial, 0)
        else:
            lax.fori_loop(0, depth, prepare, 0)
        for copy in copies:
            copy.wait_recv()
        started.extend(copies)
        columns = psi_yr[step]
        for side, z_at in ((0, 16), (1, 17 + depth)):
            plane_in = psi_zy[step, side]
            columns = jnp.where(lane == z_at, pltpu.roll(plane_in, z_at + 1, 1), columns)
            columns = jnp.where(lane == z_at + 48, pltpu.roll(plane_in, z_at + 48, 1), columns)
        psi_yr[step] = columns
        rows_lane = lax.broadcasted_iota(jnp.int32, (depth + 2 * PAD, breadth), 1)
        for side in range(2):
            own, other = psi_xr[step, side], psi_xyr[step, side]
            psi_rows[0, side] = pltpu.roll(jnp.where(rows_lane == last, other, own), 1, 1)
            psi_rows[1, side] = pltpu.roll(jnp.where(rows_lane == 0, other, own), last, 1)

        def differences(p, carry):
            value = psi[step, p]
            columns = psi_yr[step]
            at = pl.ds(p + PAD - 1, 1)
            y_low = jnp.where(
                lane == 0, pltpu.roll(columns, 112 - p, 1), pltpu.roll(value, 1, 1)
            )
            y_high = jnp.where(
                lane == last, pltpu.roll(columns, 63 - p, 1), pltpu.roll(value, last, 1)
            )
            y_sum, y_diff = y_high + y_low, y_high - y_low
            x_low = from_low_x(value, psi_xr[step, 0, at, :])
            x_high = from_high_x(value, psi_xr[step, 1, at, :])
            edges = [
                [psi_rows[s, side, at, :] for s in range(2)] for side in range(2)
            ]
            x_diff = x_high - x_low
            field_a[p] = 2.0 * value + (x_high + x_low) + y_sum
            field_dx[p] = x_diff
            field_dy[p] = y_diff
            field_gx[p] = (
                2.0 * x_diff
                + from_high_x(y_sum, edges[1][1] + edges[1][0])
                - from_low_x(y_sum, edges[0][1] + edges[0][0])
            )
            field_gy[p] = (
                2.0 * y_diff
                + from_high_x(y_diff, edges[1][1] - edges[1][0])
                + from_low_x(y_diff, edges[0][1] - edges[0][0])
            )
            return carry

        lax.fori_loop(0, depth + 2, differences, 0, unroll=2)

        def collide(z, packs):
            p = z + 1
            scale = (coupling / 36.0) * psi[step, p]
            force = [
                scale * (field_a[p + 1] - field_a[p - 1]),
                scale * (field_gx[p] + (field_dx[p + 1] + field_dx[p - 1])),
                scale * (field_gy[p] + (field_dy[p + 1] + field_dy[p - 1])),
            ]
            density = moments[0, z]
            momentum = [moments[1 + a, z] for a in range(3)]
            speed = [speeds[a, z] for a in range(3)]
            post = [m + f for m, f in zip(momentum, force)]
            second = {}
            for k, (a, b) in enumerate(pair_list):
                value = moments[4 + k, z] + (speed[a] * force[b] + force[a] * speed[b])
                second[a, b] = value * (0.125 if a == b else 0.25)
            flow = [m * (1.0 / 12.0) for m in post]
            base = density * (1.0 / 36.0) - (
                second[0, 0] + second[1, 1] + second[2, 2]
            ) * (1.0 / 3.0)
            value_of = {(0, 0, 0): 12.0 * base}
            for a in range(3):
                even = 2.0 * (base + second[a, a])
                odd = 2.0 * flow[a]
                for sign in (1, -1):
                    vector = [0, 0, 0]
                    vector[a] = sign
                    value_of[tuple(vector)] = even + odd if sign == 1 else even - odd
            for a, b in pair_list[3:]:
                both = base + (second[a, a] + second[b, b])
                for sign in (1, -1):
                    if sign == 1:
                        even, odd = both + second[a, b], flow[a] + flow[b]
                    else:
                        even, odd = both - second[a, b], flow[a] - flow[b]
                    vector = [0, 0, 0]
                    vector[a], vector[b] = 1, sign
                    value_of[tuple(vector)] = even + odd
                    vector[a], vector[b] = -1, -sign
                    value_of[tuple(vector)] = even - odd
            for index, vector in enumerate(vectors):
                pops[step, index, p] = value_of[vector]
            for k in range(5):
                pop_rows[0, k, pl.ds(z, 1), :] = value_of[x_lists[0][k]][width - 1 : width]
                pop_rows[1, k, pl.ds(z, 1), :] = value_of[x_lists[1][k]][0:1]
            up, down = packs
            for k in range(5):
                at = p + 18 * k
                up = jnp.where(lane == at, pltpu.roll(value_of[y_lists[0][k]], at + 1, 1), up)
                down = jnp.where(lane == at, pltpu.roll(value_of[y_lists[1][k]], at, 1), down)
            return up, down

        nothing = jnp.zeros((width, breadth), jnp.float32)
        up, down = lax.fori_loop(0, depth, collide, (nothing, nothing))
        pop_ys[step, 0] = up
        pop_ys[step, 1] = down
        for k in range(5):
            pop_zs[step, 0, k] = pops[step, k, depth].astype(jnp.bfloat16)
            pop_zs[step, 1, k] = pops[step, 5 + k, 1].astype(jnp.bfloat16)
            for side in range(2):
                pop_xs[step, side, k] = pop_rows[side, k].astype(jnp.bfloat16)
        two = pl.ds(3, 2)
        copies = start(1, step, [
            (pop_xs.at[step, 0, 1], pop_zxr.at[step, 0, 0]),
            (pop_xs.at[step, 0, 2], pop_zxr.at[step, 0, 1]),
            (pop_xs.at[step, 1, 1], pop_zxr.at[step, 1, 0]),
            (pop_xs.at[step, 1, 2], pop_zxr.at[step, 1, 1]),
            (pop_xs.at[step, 0], pop_xin.at[step, 0]),
            (pop_xs.at[step, 1], pop_xin.at[step, 1]),
            (pop_xs.at[step, 0, two], pop_xyr.at[step, 0]),
            (pop_xs.at[step, 1, two], pop_xyr.at[step, 1]),
            (pop_zs.at[step, 0], pop_zin.at[step, 0]),
            (pop_zs.at[step, 1], pop_zin.at[step, 1]),
            (pop_zs.at[step, 0, two], pop_zy.at[step, 0]),
            (pop_zs.at[step, 1, two], pop_zy.at[step, 1]),
            (pop_ys.at[step], pop_yr.at[step]),
        ])

        def stream(z, carry):
            up, down = pop_yr[step, 0], pop_yr[step, 1]
            passed = {}
            for index, vector in enumerate(vectors):
                p = z + 1 - vector[0]
                value = pops[step, index, p]
                if vector[2] == 1:
                    at = p + 18 * y_lists[0].index(vector)
                    value = jnp.where(
                        lane == 0, pltpu.roll(up, 128 - at, 1), pltpu.roll(value, 1, 1)
                    )
                elif vector[2] == -1:
                    at = p + 18 * y_lists[1].index(vector)
                    value = jnp.where(
                        lane == last, pltpu.roll(down, 127 - at, 1), pltpu.roll(value, last, 1)
                    )
                if vector[1] == 1:
                    value = from_low_x(value, 0.0)
                elif vector[1] == -1:
                    value = from_high_x(value, 0.0)
                passed[vector] = value
            totals, moved = {}, {}
            for a in range(3):
                vector = [0, 0, 0]
                vector[a] = 1
                plus = passed[tuple(vector)]
                vector[a] = -1
                minus = passed[tuple(vector)]
                totals[a], moved[a] = plus + minus, plus - minus
            axis_sum = totals[0] + totals[1] + totals[2]
            cross, pair_sum = {}, {}
            for a, b in pair_list[3:]:
                found = {}
                for sign_a in (1, -1):
                    for sign_b in (1, -1):
                        vector = [0, 0, 0]
                        vector[a], vector[b] = sign_a, sign_b
                        found[sign_a, sign_b] = passed[tuple(vector)]
                same = found[1, 1] + found[-1, -1]
                mixed = found[1, -1] + found[-1, 1]
                same_odd = found[1, 1] - found[-1, -1]
                mixed_odd = found[1, -1] - found[-1, 1]
                cross[a, b] = same - mixed
                pair_sum[a, b] = same + mixed
                moved[a] = moved[a] + (same_odd + mixed_odd)
                moved[b] = moved[b] + (same_odd - mixed_odd)
            moments[0, z] = passed[0, 0, 0] + axis_sum + (
                pair_sum[0, 1] + pair_sum[0, 2] + pair_sum[1, 2]
            )
            for a in range(3):
                moments[1 + a, z] = moved[a]
            moments[4, z] = totals[0] + (pair_sum[0, 1] + pair_sum[0, 2])
            moments[5, z] = totals[1] + (pair_sum[0, 1] + pair_sum[1, 2])
            moments[6, z] = totals[2] + (pair_sum[0, 2] + pair_sum[1, 2])
            for k, pair in enumerate(pair_list[3:]):
                moments[7 + k, z] = cross[pair]
            return carry

        copies[-1].wait_recv()
        lax.fori_loop(1, depth - 1, stream, 0)
        for copy in copies[:-1]:
            copy.wait_recv()
        started.extend(copies)
        f32 = jnp.float32
        for k in range(5):
            pops[step, k, 0] = pop_zin[step, 0, k].astype(f32)
            pops[step, 5 + k, depth + 1] = pop_zin[step, 1, k].astype(f32)
        far = 36 + depth + 1
        corner = [[pop_zy[step, side, k].astype(f32) for k in range(2)] for side in range(2)]
        up, down = pop_yr[step, 0], pop_yr[step, 1]
        up = jnp.where(lane == 18, pltpu.roll(corner[0][0], 19, 1), up)
        down = jnp.where(lane == 18, pltpu.roll(corner[0][1], 18, 1), down)
        up = jnp.where(lane == far, pltpu.roll(corner[1][0], far + 1, 1), up)
        down = jnp.where(lane == far, pltpu.roll(corner[1][1], far, 1), down)
        pop_yr[step, 0] = up
        pop_yr[step, 1] = down
        lax.fori_loop(0, 2, lambda i, carry: stream(i * (depth - 1), carry), 0)

        z_row = lax.broadcasted_iota(jnp.int32, (depth, breadth), 0)
        z_lane = lax.broadcasted_iota(jnp.int32, (depth, breadth), 1)
        for side in range(2):
            own = [pop_xin[step, side, k].astype(f32) for k in range(5)]
            edge = [pop_zxr[step, side, k].astype(f32) for k in range(2)]
            other = [pop_xyr[step, side, k].astype(f32) for k in range(2)]
            plain = own[0]
            z_up = jnp.where(z_row == 0, pltpu.roll(edge[0], 1, 0), pltpu.roll(own[1], 1, 0))
            z_down = jnp.where(
                z_row == depth - 1,
                pltpu.roll(edge[1], depth - 1, 0),
                pltpu.roll(own[2], depth - 1, 0),
            )
            y_up = pltpu.roll(jnp.where(z_lane == last, other[0], own[3]), 1, 1)
            y_down = pltpu.roll(jnp.where(z_lane == 0, other[1], own[4]), last, 1)
            z_even, z_odd = z_up + z_down, z_up - z_down
            y_even, y_odd = y_up + y_down, y_up - y_down
            total = plain + (z_even + y_even)
            if side == 0:
                adds = [total, z_odd, total, y_odd, z_even, total, y_even, z_odd, y_odd]
            else:
                adds = [total, z_odd, -total, y_odd, z_even, total, y_even, -z_odd, -y_odd]
            for k, add in enumerate(adds):
                side_sums[side, k] = add

        def add_sides(z, carry):
            at = pl.ds(z, 1)
            for k, c in enumerate((0, 1, 2, 3, 4, 5, 6, 7, 9)):
                for side, x in ((0, 0), (1, width - 1)):
                    cells = (c, z, pl.ds(x, 1), slice(None))
                    moments[cells] = moments[cells] + side_sums[side, k, at, :]
            return carry

        if step < STEPS - 1:
            lax.fori_loop(0, depth, add_sides, 0)

    moves = []
    for g in range(groups):
        lax.fori_loop(g * group_z, (g + 1) * group_z, add_sides, 0)
        block = jnp.concatenate(
            [
                moments[c, g * group_z : (g + 1) * group_z]
                .reshape(group_z * width, breadth)
                .astype(jnp.bfloat16)
                for c in range(10)
            ],
            axis=1,
        )
        rows = jnp.dot(order, block, preferred_element_type=jnp.float32).astype(jnp.bfloat16)
        for c in range(10):
            sent[g, :, c] = rows[:, c * breadth : (c + 1) * breadth].reshape(
                planes, tile, breadth
            )
        for k in range(planes - 1, 0, -1):
            copy = pltpu.make_async_remote_copy(
                src_ref=sent.at[g, lax.rem(me_x + k, planes)],
                dst_ref=arrived.at[g, k],
                send_sem=move_send.at[g, k],
                recv_sem=move_recv.at[g, k],
                device_id=device((0, k, 0)),
                device_id_type=MESH,
            )
            copy.start()
            moves.append((g, copy))
        arrived[g, 0] = sent[g, me_x]

    for copy in started:
        copy.wait_send()

    for copy in info_copies:
        copy.wait()
    slots = planes * tile
    parts = [info[me_x, 0:1, 0:tile]]
    for k in range(1, planes):
        parts.append(info_in[k, 0:1, 0:tile])
    place = jnp.concatenate(parts, axis=1)
    to_row = lax.broadcasted_iota(jnp.int32, (group_z * width, slots), 0)
    from_slot = lax.broadcasted_iota(jnp.int32, (group_z * width, slots), 1)
    fits = (place == lax.rem(to_row, width).astype(jnp.float32)) & (
        lax.rem(from_slot, tile) // capacity == to_row // width
    )
    placing = jnp.where(fits, 1.0, 0.0).astype(jnp.bfloat16)
    for g in range(groups):
        for held, copy in moves:
            if held == g:
                copy.wait()

        block = jnp.concatenate(
            [arrived[g, :, c].reshape(slots, breadth) for c in range(10)], axis=1
        )
        rows = jnp.dot(placing, block, preferred_element_type=jnp.float32).astype(jnp.bfloat16)
        for c in range(10):
            out[c, pl.ds(g * group_z, group_z)] = rows[
                :, c * breadth : (c + 1) * breadth
            ].reshape(group_z, width, breadth)


def shards(mesh_sizes, phase, velocity, stress, new_slot):
    normal, planes = mesh_sizes
    depth, width, breadth = phase.shape
    capacity = 2 * ((width // 2 + planes - 1) // planes)
    group_z = 16 // capacity
    groups = depth // group_z
    plane = (width, breadth)
    padded = (depth + 2 * PAD, breadth)
    f32, bf16 = jnp.float32, jnp.bfloat16
    vmem = pltpu.VMEM
    dma = pltpu.SemaphoreType.DMA
    whole = pl.BlockSpec(memory_space=pltpu.VMEM)
    return pl.pallas_call(
        functools.partial(kernel, (normal, planes, group_z, depth, width, breadth)),
        out_shape=jax.ShapeDtypeStruct((10, depth, width, breadth), bf16),
        in_specs=[pl.BlockSpec(memory_space=pltpu.HBM)] * 3
        + [pl.BlockSpec(memory_space=pltpu.SMEM)],
        out_specs=whole,
        scratch_shapes=[
            vmem((depth,) + plane, jnp.int32),
            vmem((3, depth) + plane, f32),
            vmem((6, depth) + plane, f32),
            vmem((10, depth) + plane, f32),
            vmem((3, depth) + plane, f32),
            vmem((STEPS, depth + 2) + plane, f32),
            vmem((STEPS, 2, depth, breadth), f32),
            vmem((STEPS, 2) + padded, f32),
            vmem((STEPS, 2) + padded, f32),
            vmem((STEPS,) + plane, f32),
            vmem((STEPS,) + plane, f32),
            vmem((STEPS, 2) + plane, f32),
            vmem((2, 2) + padded, f32),
        ]
        + [vmem((depth + 2,) + plane, f32)] * 5
        + [
            vmem((STEPS, 19, depth + 2) + plane, f32),
            vmem((2, 5, depth, breadth), f32),
            vmem((STEPS, 2, 5, depth, breadth), bf16),
            vmem((STEPS, 2, 5, depth, breadth), bf16),
            vmem((STEPS, 2, 2, depth, breadth), bf16),
            vmem((STEPS, 2, 2, depth, breadth), bf16),
            vmem((STEPS, 2) + plane, f32),
            vmem((STEPS, 2) + plane, f32),
            vmem((STEPS, 2, 5) + plane, bf16),
            vmem((STEPS, 2, 5) + plane, bf16),
            vmem((STEPS, 2, 2) + plane, bf16),
            vmem((2, 9, depth, breadth), f32),
            vmem((groups, planes, 10, 16, breadth), bf16),
            vmem((groups, planes, 10, 16, breadth), bf16),
            vmem((planes, 8, 128), f32),
            vmem((planes, 8, 128), f32),
            dma((3,)),
            dma((2, STEPS, 13)),
            dma((2, STEPS, 13)),
            dma((groups, planes)),
            dma((groups, planes)),
            dma((planes,)),
            dma((planes,)),
        ],
        compiler_params=pltpu.CompilerParams(
            collective_id=0, has_side_effects=True, vmem_limit_bytes=56 * 1024 * 1024
        ),
    )(phase, velocity, stress, new_slot)


def solution(mesh):
    placed = (
        P(("groups", "normal"), "plane", "inner"),
        P(None, ("groups", "normal"), "plane", "inner"),
        P(None, ("groups", "normal"), "plane", "inner"),
        P(("groups", "plane")),
    )
    return jax.shard_map(
        functools.partial(shards, (mesh.shape["normal"], mesh.shape["plane"])),
        mesh=mesh,
        in_specs=placed,
        out_specs=P(None, ("groups", "normal"), "plane", "inner"),
        check_vma=False,
    )
```

```python
import functools

import jax
import jax.numpy as jnp
from jax import lax
from jax.experimental import pallas as pl
from jax.experimental.pallas import tpu as pltpu
from jax.sharding import PartitionSpec as P

STEPS = 2
MESH = pl.DeviceIdType.MESH
coupling = 1.5

vectors = (
    (1, 0, 0), (1, 1, 0), (1, -1, 0), (1, 0, 1), (1, 0, -1),
    (-1, 0, 0), (-1, 1, 0), (-1, -1, 0), (-1, 0, 1), (-1, 0, -1),
    (0, 1, 0), (0, -1, 0), (0, 0, 1), (0, 0, -1),
    (0, 1, 1), (0, 1, -1), (0, -1, 1), (0, -1, -1),
    (0, 0, 0),
)
x_lists = tuple(
    ((0, s, 0), (1, s, 0), (-1, s, 0), (0, s, 1), (0, s, -1)) for s in (1, -1)
)
y_lists = tuple(
    ((0, 0, s), (1, 0, s), (-1, 0, s), (0, 1, s), (0, -1, s)) for s in (1, -1)
)
pair_list = ((0, 0), (1, 1), (2, 2), (0, 1), (0, 2), (1, 2))
PAD = 8


def kernel(
    sizes, phase_hbm, velocity_hbm, stress_hbm, new_slot_hbm, out,
    new_slot, phase, velocity, stress, moments, speeds, psi, psi_xs, psi_xr, psi_xyr, psi_ys, psi_yr, psi_zy, psi_rows,
    field_a, field_dx, field_dy, field_gx, field_gy,
    pops, pop_rows, pop_xs, pop_xin, pop_xyr, pop_zxr, pop_ys, pop_yr,
    pop_zs, pop_zin, pop_zy, side_sums, sent, arrived, info, info_in,
    load_sem, send_sem, recv_sem, move_send, move_recv, info_send, info_recv,
):
    normal, planes, group_z, depth, width, breadth = sizes
    groups = depth // group_z
    me_z = lax.axis_index("normal")
    me_x = lax.axis_index("plane")
    me_y = lax.axis_index("inner")

    def device(offset):
        place = {}
        if offset[0] % normal:
            place["normal"] = lax.rem(me_z + offset[0] % normal, normal)
        if offset[1] % planes:
            place["plane"] = lax.rem(me_x + offset[1] % planes, planes)
        if offset[2] % 2:
            place["inner"] = 1 - me_y
        return place

    around = [
        (1, 1, 0), (-1, 1, 0), (1, -1, 0), (-1, -1, 0),
        (0, 1, 0), (0, -1, 0), (0, 1, 1), (0, -1, 1),
        (1, 0, 0), (-1, 0, 0), (1, 0, 1), (-1, 0, 1), (0, 0, 1),
    ]
    partners = []
    for a, b, c in around + [(0, k, 0) for k in range(1, planes)]:
        offset = (a % normal, b % planes, c % 2)
        if offset not in partners:
            partners.append(offset)
    loads = [
        pltpu.make_async_copy(source, target, load_sem.at[number])
        for number, (source, target) in enumerate(
            ((phase_hbm, phase), (velocity_hbm, velocity), (stress_hbm, stress),
             (new_slot_hbm, new_slot))
        )
    ]
    for load in loads:
        load.start()
    barrier = pltpu.get_barrier_semaphore()
    for offset in partners:
        pl.semaphore_signal(barrier, inc=1, device_id=device(offset), device_id_type=MESH)

    lane = lax.broadcasted_iota(jnp.int32, (width, breadth), 1)
    row = lax.broadcasted_iota(jnp.int32, (width, breadth), 0)
    last = breadth - 1

    def start(kind, step, pairs):
        copies = []
        for number, (offset, (source, target)) in enumerate(zip(around, pairs)):
            copy = pltpu.make_async_remote_copy(
                src_ref=source,
                dst_ref=target,
                send_sem=send_sem.at[kind, step, number],
                recv_sem=recv_sem.at[kind, step, number],
                device_id=device(offset),
                device_id_type=MESH,
            )
            copy.start()
            copies.append(copy)
        return copies

    def from_low_x(value, edge):
        return jnp.where(row == 0, edge, pltpu.roll(value, 1, 0))

    def from_high_x(value, edge):
        return jnp.where(row == width - 1, edge, pltpu.roll(value, width - 1, 0))

    def initial(z, carry):
        density = moments[0, z]
        speed = [velocity[a, z] for a in range(3)]
        momentum = [density * s for s in speed]
        for a in range(3):
            moments[1 + a, z] = momentum[a]
            speeds[a, z] = speed[a]
        for k, (a, b) in enumerate(pair_list):
            moments[4 + k, z] = momentum[a] * speed[b] + 0.375 * stress[k, z]
        return carry

    def prepare(z, carry):
        density = moments[0, z]
        inverse = 1.0 / density
        momentum = [moments[1 + a, z] for a in range(3)]
        speed = [m * inverse for m in momentum]
        eighth = 0.125 * density
        for a in range(3):
            speeds[a, z] = speed[a]
        for k, (a, b) in enumerate(pair_list):
            value = 0.625 * (momentum[a] * speed[b]) + 0.375 * moments[4 + k, z]
            moments[4 + k, z] = value - eighth if a == b else value
        return carry

    def start_density(z, carry):
        moments[0, z] = jnp.where(phase[z] == 1, 2.0, 0.3).astype(jnp.float32)
        return carry

    loads[0].wait()
    lax.fori_loop(0, depth, start_density, 0, unroll=4)

    tile = 16
    capacity = tile // group_z
    info_copies = []

    def plan():
        slots = planes * tile
        blocks = [new_slot[x] for x in range(width)]
        owners = [lax.div(block, width) for block in blocks]
        places = [lax.rem(block, width) for block in blocks]
        at_slot = []
        for x in range(width):
            earlier = jnp.int32(0)
            for other in range(x):
                earlier = earlier + jnp.where(owners[other] == owners[x], 1, 0)
            at_slot.append(owners[x] * capacity + earlier)
        shape = (slots, group_z * width)
        to_slot = lax.broadcasted_iota(jnp.int32, shape, 0)
        from_cell = lax.broadcasted_iota(jnp.int32, shape, 1)
        from_x = lax.rem(from_cell[0:8], width)
        slot_of = jnp.zeros(from_x.shape, jnp.int32)
        for x in range(width):
            slot_of = jnp.where(from_x == x, at_slot[x], slot_of)
        here = lax.div(to_slot, tile) * capacity + lax.rem(to_slot, capacity)
        layer = lax.div(lax.rem(to_slot, tile), capacity)
        chosen = (slot_of[0:1] == here) & (layer == lax.div(from_cell, width))
        order = jnp.where(chosen, 1.0, 0.0).astype(jnp.bfloat16)
        small = lax.broadcasted_iota(jnp.int32, (8, 128), 1)
        for t in range(planes):
            wanted = lax.rem(small, capacity) + t * capacity
            place = jnp.full((8, 128), -1, jnp.int32)
            for x in range(width):
                place = jnp.where(wanted == at_slot[x], places[x], place)
            info[t] = place.astype(jnp.float32)
        return order

    def send_info():
        for k in range(1, planes):
            copy = pltpu.make_async_remote_copy(
                src_ref=info.at[lax.rem(me_x + k, planes)],
                dst_ref=info_in.at[k],
                send_sem=info_send.at[k],
                recv_sem=info_recv.at[k],
                device_id=device((0, k, 0)),
                device_id_type=MESH,
            )
            copy.start()
            info_copies.append(copy)

    loads[3].wait()
    order = plan()
    started = []
    for step in range(STEPS):
        def potential(z, packed):
            value = 1.0 - jnp.exp(-moments[0, z])
            psi[step, z + 1] = value
            psi_xs[step, 0, pl.ds(z, 1), :] = value[width - 1 : width]
            psi_xs[step, 1, pl.ds(z, 1), :] = value[0:1]
            packed = jnp.where(lane == z + 17, pltpu.roll(value, z + 18, 1), packed)
            return jnp.where(lane == z + 65, pltpu.roll(value, z + 65, 1), packed)

        psi_ys[step] = lax.fori_loop(
            0, depth, potential, jnp.zeros((width, breadth), jnp.float32), unroll=4
        )
        low, high = pl.ds(0, PAD), pl.ds(depth - PAD, PAD)
        inner_rows = pl.ds(PAD, depth)
        before, after = pl.ds(0, PAD), pl.ds(depth + PAD, PAD)
        if step == 0:
            pl.semaphore_wait(barrier, len(partners))
        copies = start(0, step, [
            (psi_xs.at[step, 0, high], psi_xr.at[step, 0, before]),
            (psi_xs.at[step, 0, low], psi_xr.at[step, 0, after]),
            (psi_xs.at[step, 1, high], psi_xr.at[step, 1, before]),
            (psi_xs.at[step, 1, low], psi_xr.at[step, 1, after]),
            (psi_xs.at[step, 0], psi_xr.at[step, 0, inner_rows]),
            (psi_xs.at[step, 1], psi_xr.at[step, 1, inner_rows]),
            (psi_xs.at[step, 0], psi_xyr.at[step, 0, inner_rows]),
            (psi_xs.at[step, 1], psi_xyr.at[step, 1, inner_rows]),
            (psi.at[step, depth], psi.at[step, 0]),
            (psi.at[step, 1], psi.at[step, depth + 1]),
            (psi.at[step, depth], psi_zy.at[step, 0]),
            (psi.at[step, 1], psi_zy.at[step, 1]),
            (psi_ys.at[step], psi_yr.at[step]),
        ])
        if step == 0:
            send_info()
            loads[1].wait()
            loads[2].wait()
            lax.fori_loop(0, depth, initial, 0)
        else:
            lax.fori_loop(0, depth, prepare, 0, unroll=4)
        for copy in copies:
            copy.wait_recv()
        started.extend(copies)
        columns = psi_yr[step]
        for side, z_at in ((0, 16), (1, 17 + depth)):
            plane_in = psi_zy[step, side]
            columns = jnp.where(lane == z_at, pltpu.roll(plane_in, z_at + 1, 1), columns)
            columns = jnp.where(lane == z_at + 48, pltpu.roll(plane_in, z_at + 48, 1), columns)
        psi_yr[step] = columns
        rows_lane = lax.broadcasted_iota(jnp.int32, (depth + 2 * PAD, breadth), 1)
        for side in range(2):
            own, other = psi_xr[step, side], psi_xyr[step, side]
            psi_rows[0, side] = pltpu.roll(jnp.where(rows_lane == last, other, own), 1, 1)
            psi_rows[1, side] = pltpu.roll(jnp.where(rows_lane == 0, other, own), last, 1)

        def differences(p, carry):
            value = psi[step, p]
            columns = psi_yr[step]
            at = pl.ds(p + PAD - 1, 1)
            y_low = jnp.where(
                lane == 0, pltpu.roll(columns, 112 - p, 1), pltpu.roll(value, 1, 1)
            )
            y_high = jnp.where(
                lane == last, pltpu.roll(columns, 63 - p, 1), pltpu.roll(value, last, 1)
            )
            y_sum, y_diff = y_high + y_low, y_high - y_low
            x_low = from_low_x(value, psi_xr[step, 0, at, :])
            x_high = from_high_x(value, psi_xr[step, 1, at, :])
            edges = [
                [psi_rows[s, side, at, :] for s in range(2)] for side in range(2)
            ]
            x_diff = x_high - x_low
            field_a[p] = 2.0 * value + (x_high + x_low) + y_sum
            field_dx[p] = x_diff
            field_dy[p] = y_diff
            field_gx[p] = (
                2.0 * x_diff
                + from_high_x(y_sum, edges[1][1] + edges[1][0])
                - from_low_x(y_sum, edges[0][1] + edges[0][0])
            )
            field_gy[p] = (
                2.0 * y_diff
                + from_high_x(y_diff, edges[1][1] - edges[1][0])
                + from_low_x(y_diff, edges[0][1] - edges[0][0])
            )
            return carry

        lax.fori_loop(0, depth + 2, differences, 0, unroll=3)

        def collide(z, packs):
            p = z + 1
            scale = (coupling / 36.0) * psi[step, p]
            force = [
                scale * (field_a[p + 1] - field_a[p - 1]),
                scale * (field_gx[p] + (field_dx[p + 1] + field_dx[p - 1])),
                scale * (field_gy[p] + (field_dy[p + 1] + field_dy[p - 1])),
            ]
            density = moments[0, z]
            momentum = [moments[1 + a, z] for a in range(3)]
            speed = [speeds[a, z] for a in range(3)]
            post = [m + f for m, f in zip(momentum, force)]
            second = {}
            for k, (a, b) in enumerate(pair_list):
                value = moments[4 + k, z] + (speed[a] * force[b] + force[a] * speed[b])
                second[a, b] = value * (0.125 if a == b else 0.25)
            flow = [m * (1.0 / 12.0) for m in post]
            base = density * (1.0 / 36.0) - (
                second[0, 0] + second[1, 1] + second[2, 2]
            ) * (1.0 / 3.0)
            value_of = {(0, 0, 0): 12.0 * base}
            for a in range(3):
                even = 2.0 * (base + second[a, a])
                odd = 2.0 * flow[a]
                for sign in (1, -1):
                    vector = [0, 0, 0]
                    vector[a] = sign
                    value_of[tuple(vector)] = even + odd if sign == 1 else even - odd
            for a, b in pair_list[3:]:
                both = base + (second[a, a] + second[b, b])
                for sign in (1, -1):
                    if sign == 1:
                        even, odd = both + second[a, b], flow[a] + flow[b]
                    else:
                        even, odd = both - second[a, b], flow[a] - flow[b]
                    vector = [0, 0, 0]
                    vector[a], vector[b] = 1, sign
                    value_of[tuple(vector)] = even + odd
                    vector[a], vector[b] = -1, -sign
                    value_of[tuple(vector)] = even - odd
            for index, vector in enumerate(vectors):
                pops[step, index, p] = value_of[vector]
            for k in range(5):
                pop_rows[0, k, pl.ds(z, 1), :] = value_of[x_lists[0][k]][width - 1 : width]
                pop_rows[1, k, pl.ds(z, 1), :] = value_of[x_lists[1][k]][0:1]
            up, down = packs
            for k in range(5):
                at = p + 18 * k
                up = jnp.where(lane == at, pltpu.roll(value_of[y_lists[0][k]], at + 1, 1), up)
                down = jnp.where(lane == at, pltpu.roll(value_of[y_lists[1][k]], at, 1), down)
            return up, down

        nothing = jnp.zeros((width, breadth), jnp.float32)
        up, down = lax.fori_loop(0, depth, collide, (nothing, nothing), unroll=4)
        pop_ys[step, 0] = up
        pop_ys[step, 1] = down
        for k in range(5):
            pop_zs[step, 0, k] = pops[step, k, depth].astype(jnp.bfloat16)
            pop_zs[step, 1, k] = pops[step, 5 + k, 1].astype(jnp.bfloat16)
            for side in range(2):
                pop_xs[step, side, k] = pop_rows[side, k].astype(jnp.bfloat16)
        two = pl.ds(3, 2)
        copies = start(1, step, [
            (pop_xs.at[step, 0, 1], pop_zxr.at[step, 0, 0]),
            (pop_xs.at[step, 0, 2], pop_zxr.at[step, 0, 1]),
            (pop_xs.at[step, 1, 1], pop_zxr.at[step, 1, 0]),
            (pop_xs.at[step, 1, 2], pop_zxr.at[step, 1, 1]),
            (pop_xs.at[step, 0], pop_xin.at[step, 0]),
            (pop_xs.at[step, 1], pop_xin.at[step, 1]),
            (pop_xs.at[step, 0, two], pop_xyr.at[step, 0]),
            (pop_xs.at[step, 1, two], pop_xyr.at[step, 1]),
            (pop_zs.at[step, 0], pop_zin.at[step, 0]),
            (pop_zs.at[step, 1], pop_zin.at[step, 1]),
            (pop_zs.at[step, 0, two], pop_zy.at[step, 0]),
            (pop_zs.at[step, 1, two], pop_zy.at[step, 1]),
            (pop_ys.at[step], pop_yr.at[step]),
        ])

        def stream(z, carry):
            up, down = pop_yr[step, 0], pop_yr[step, 1]
            passed = {}
            for index, vector in enumerate(vectors):
                p = z + 1 - vector[0]
                value = pops[step, index, p]
                if vector[2] == 1:
                    at = p + 18 * y_lists[0].index(vector)
                    value = jnp.where(
                        lane == 0, pltpu.roll(up, 128 - at, 1), pltpu.roll(value, 1, 1)
                    )
                elif vector[2] == -1:
                    at = p + 18 * y_lists[1].index(vector)
                    value = jnp.where(
                        lane == last, pltpu.roll(down, 127 - at, 1), pltpu.roll(value, last, 1)
                    )
                if vector[1] == 1:
                    value = from_low_x(value, 0.0)
                elif vector[1] == -1:
                    value = from_high_x(value, 0.0)
                passed[vector] = value
            totals, moved = {}, {}
            for a in range(3):
                vector = [0, 0, 0]
                vector[a] = 1
                plus = passed[tuple(vector)]
                vector[a] = -1
                minus = passed[tuple(vector)]
                totals[a], moved[a] = plus + minus, plus - minus
            axis_sum = totals[0] + totals[1] + totals[2]
            cross, pair_sum = {}, {}
            for a, b in pair_list[3:]:
                found = {}
                for sign_a in (1, -1):
                    for sign_b in (1, -1):
                        vector = [0, 0, 0]
                        vector[a], vector[b] = sign_a, sign_b
                        found[sign_a, sign_b] = passed[tuple(vector)]
                same = found[1, 1] + found[-1, -1]
                mixed = found[1, -1] + found[-1, 1]
                same_odd = found[1, 1] - found[-1, -1]
                mixed_odd = found[1, -1] - found[-1, 1]
                cross[a, b] = same - mixed
                pair_sum[a, b] = same + mixed
                moved[a] = moved[a] + (same_odd + mixed_odd)
                moved[b] = moved[b] + (same_odd - mixed_odd)
            moments[0, z] = passed[0, 0, 0] + axis_sum + (
                pair_sum[0, 1] + pair_sum[0, 2] + pair_sum[1, 2]
            )
            for a in range(3):
                moments[1 + a, z] = moved[a]
            moments[4, z] = totals[0] + (pair_sum[0, 1] + pair_sum[0, 2])
            moments[5, z] = totals[1] + (pair_sum[0, 1] + pair_sum[1, 2])
            moments[6, z] = totals[2] + (pair_sum[0, 2] + pair_sum[1, 2])
            for k, pair in enumerate(pair_list[3:]):
                moments[7 + k, z] = cross[pair]
            return carry

        copies[-1].wait_recv()
        lax.fori_loop(1, depth - 1, stream, 0, unroll=7)
        for copy in copies[:-1]:
            copy.wait_recv()
        started.extend(copies)
        f32 = jnp.float32
        for k in range(5):
            pops[step, k, 0] = pop_zin[step, 0, k].astype(f32)
            pops[step, 5 + k, depth + 1] = pop_zin[step, 1, k].astype(f32)
        far = 36 + depth + 1
        corner = [[pop_zy[step, side, k].astype(f32) for k in range(2)] for side in range(2)]
        up, down = pop_yr[step, 0], pop_yr[step, 1]
        up = jnp.where(lane == 18, pltpu.roll(corner[0][0], 19, 1), up)
        down = jnp.where(lane == 18, pltpu.roll(corner[0][1], 18, 1), down)
        up = jnp.where(lane == far, pltpu.roll(corner[1][0], far + 1, 1), up)
        down = jnp.where(lane == far, pltpu.roll(corner[1][1], far, 1), down)
        pop_yr[step, 0] = up
        pop_yr[step, 1] = down
        lax.fori_loop(0, 2, lambda i, carry: stream(i * (depth - 1), carry), 0)

        z_row = lax.broadcasted_iota(jnp.int32, (depth, breadth), 0)
        z_lane = lax.broadcasted_iota(jnp.int32, (depth, breadth), 1)
        for side in range(2):
            own = [pop_xin[step, side, k].astype(f32) for k in range(5)]
            edge = [pop_zxr[step, side, k].astype(f32) for k in range(2)]
            other = [pop_xyr[step, side, k].astype(f32) for k in range(2)]
            plain = own[0]
            z_up = jnp.where(z_row == 0, pltpu.roll(edge[0], 1, 0), pltpu.roll(own[1], 1, 0))
            z_down = jnp.where(
                z_row == depth - 1,
                pltpu.roll(edge[1], depth - 1, 0),
                pltpu.roll(own[2], depth - 1, 0),
            )
            y_up = pltpu.roll(jnp.where(z_lane == last, other[0], own[3]), 1, 1)
            y_down = pltpu.roll(jnp.where(z_lane == 0, other[1], own[4]), last, 1)
            z_even, z_odd = z_up + z_down, z_up - z_down
            y_even, y_odd = y_up + y_down, y_up - y_down
            total = plain + (z_even + y_even)
            if side == 0:
                adds = [total, z_odd, total, y_odd, z_even, total, y_even, z_odd, y_odd]
            else:
                adds = [total, z_odd, -total, y_odd, z_even, total, y_even, -z_odd, -y_odd]
            for k, add in enumerate(adds):
                side_sums[side, k] = add

        def add_sides(z, carry):
            at = pl.ds(z, 1)
            for k, c in enumerate((0, 1, 2, 3, 4, 5, 6, 7, 9)):
                for side, x in ((0, 0), (1, width - 1)):
                    cells = (c, z, pl.ds(x, 1), slice(None))
                    moments[cells] = moments[cells] + side_sums[side, k, at, :]
            return carry

        if step < STEPS - 1:
            lax.fori_loop(0, depth, add_sides, 0, unroll=4)

    moves = []
    for g in range(groups):
        lax.fori_loop(g * group_z, (g + 1) * group_z, add_sides, 0, unroll=2)
        block = jnp.concatenate(
            [
                moments[c, g * group_z : (g + 1) * group_z]
                .reshape(group_z * width, breadth)
                .astype(jnp.bfloat16)
                for c in range(10)
            ],
            axis=1,
        )
        rows = jnp.dot(order, block, preferred_element_type=jnp.float32).astype(jnp.bfloat16)
        for c in range(10):
            sent[g, :, c] = rows[:, c * breadth : (c + 1) * breadth].reshape(
                planes, tile, breadth
            )
        for k in range(planes - 1, 0, -1):
            copy = pltpu.make_async_remote_copy(
                src_ref=sent.at[g, lax.rem(me_x + k, planes)],
                dst_ref=arrived.at[g, k],
                send_sem=move_send.at[g, k],
                recv_sem=move_recv.at[g, k],
                device_id=device((0, k, 0)),
                device_id_type=MESH,
            )
            copy.start()
            moves.append((g, copy))
        arrived[g, 0] = sent[g, me_x]

    for copy in started:
        copy.wait_send()

    for copy in info_copies:
        copy.wait()
    slots = planes * tile
    parts = [info[me_x, 0:1, 0:tile]]
    for k in range(1, planes):
        parts.append(info_in[k, 0:1, 0:tile])
    place = jnp.concatenate(parts, axis=1)
    to_row = lax.broadcasted_iota(jnp.int32, (group_z * width, slots), 0)
    from_slot = lax.broadcasted_iota(jnp.int32, (group_z * width, slots), 1)
    fits = (place == lax.rem(to_row, width).astype(jnp.float32)) & (
        lax.rem(from_slot, tile) // capacity == to_row // width
    )
    placing = jnp.where(fits, 1.0, 0.0).astype(jnp.bfloat16)
    for g in range(groups):
        for held, copy in moves:
            if held == g:
                copy.wait()

        block = jnp.concatenate(
            [arrived[g, :, c].reshape(slots, breadth) for c in range(10)], axis=1
        )
        rows = jnp.dot(placing, block, preferred_element_type=jnp.float32).astype(jnp.bfloat16)
        for c in range(10):
            out[c, pl.ds(g * group_z, group_z)] = rows[
                :, c * breadth : (c + 1) * breadth
            ].reshape(group_z, width, breadth)


def shards(mesh_sizes, phase, velocity, stress, new_slot):
    normal, planes = mesh_sizes
    depth, width, breadth = phase.shape
    capacity = 2 * ((width // 2 + planes - 1) // planes)
    group_z = 16 // capacity
    groups = depth // group_z
    plane = (width, breadth)
    padded = (depth + 2 * PAD, breadth)
    f32, bf16 = jnp.float32, jnp.bfloat16
    vmem = pltpu.VMEM
    dma = pltpu.SemaphoreType.DMA
    whole = pl.BlockSpec(memory_space=pltpu.VMEM)
    return pl.pallas_call(
        functools.partial(kernel, (normal, planes, group_z, depth, width, breadth)),
        out_shape=jax.ShapeDtypeStruct((10, depth, width, breadth), bf16),
        in_specs=[pl.BlockSpec(memory_space=pltpu.HBM)] * 4,
        out_specs=whole,
        scratch_shapes=[
            pltpu.SMEM((width,), jnp.int32),
            vmem((depth,) + plane, jnp.int32),
            vmem((3, depth) + plane, f32),
            vmem((6, depth) + plane, f32),
            vmem((10, depth) + plane, f32),
            vmem((3, depth) + plane, f32),
            vmem((STEPS, depth + 2) + plane, f32),
            vmem((STEPS, 2, depth, breadth), f32),
            vmem((STEPS, 2) + padded, f32),
            vmem((STEPS, 2) + padded, f32),
            vmem((STEPS,) + plane, f32),
            vmem((STEPS,) + plane, f32),
            vmem((STEPS, 2) + plane, f32),
            vmem((2, 2) + padded, f32),
        ]
        + [vmem((depth + 2,) + plane, f32)] * 5
        + [
            vmem((STEPS, 19, depth + 2) + plane, f32),
            vmem((2, 5, depth, breadth), f32),
            vmem((STEPS, 2, 5, depth, breadth), bf16),
            vmem((STEPS, 2, 5, depth, breadth), bf16),
            vmem((STEPS, 2, 2, depth, breadth), bf16),
            vmem((STEPS, 2, 2, depth, breadth), bf16),
            vmem((STEPS, 2) + plane, f32),
            vmem((STEPS, 2) + plane, f32),
            vmem((STEPS, 2, 5) + plane, bf16),
            vmem((STEPS, 2, 5) + plane, bf16),
            vmem((STEPS, 2, 2) + plane, bf16),
            vmem((2, 9, depth, breadth), f32),
            vmem((groups, planes, 10, 16, breadth), bf16),
            vmem((groups, planes, 10, 16, breadth), bf16),
            vmem((planes, 8, 128), f32),
            vmem((planes, 8, 128), f32),
            dma((4,)),
            dma((2, STEPS, 13)),
            dma((2, STEPS, 13)),
            dma((groups, planes)),
            dma((groups, planes)),
            dma((planes,)),
            dma((planes,)),
        ],
        compiler_params=pltpu.CompilerParams(
            collective_id=0, has_side_effects=True, vmem_limit_bytes=40 * 1024 * 1024
        ),
    )(*(pltpu.with_memory_space_constraint(x, pltpu.HBM) for x in (phase, velocity, stress, new_slot)))


def solution(mesh):
    placed = (
        P(("groups", "normal"), "plane", "inner"),
        P(None, ("groups", "normal"), "plane", "inner"),
        P(None, ("groups", "normal"), "plane", "inner"),
        P(("groups", "plane")),
    )
    return jax.shard_map(
        functools.partial(shards, (mesh.shape["normal"], mesh.shape["plane"])),
        mesh=mesh,
        in_specs=placed,
        out_specs=P(None, ("groups", "normal"), "plane", "inner"),
        check_vma=False,
    )
```

```python
import functools

import jax
import jax.numpy as jnp
from jax import lax
from jax.experimental import pallas as pl
from jax.experimental.pallas import tpu as pltpu
from jax.sharding import PartitionSpec as P

STEPS = 2
MESH = pl.DeviceIdType.MESH
coupling = 1.5

vectors = (
    (1, 0, 0), (1, 1, 0), (1, -1, 0), (1, 0, 1), (1, 0, -1),
    (-1, 0, 0), (-1, 1, 0), (-1, -1, 0), (-1, 0, 1), (-1, 0, -1),
    (0, 1, 0), (0, -1, 0), (0, 0, 1), (0, 0, -1),
    (0, 1, 1), (0, 1, -1), (0, -1, 1), (0, -1, -1),
    (0, 0, 0),
)
x_lists = tuple(
    ((0, s, 0), (1, s, 0), (-1, s, 0), (0, s, 1), (0, s, -1)) for s in (1, -1)
)
y_lists = tuple(
    ((0, 0, s), (1, 0, s), (-1, 0, s), (0, 1, s), (0, -1, s)) for s in (1, -1)
)
pair_list = ((0, 0), (1, 1), (2, 2), (0, 1), (0, 2), (1, 2))
PAD = 8


def kernel(
    sizes, phase_hbm, velocity_hbm, stress_hbm, new_slot_hbm, out,
    new_slot, phase, velocity, stress, moments, speeds, psi, psi_xs, psi_xr, psi_xyr, psi_ys, psi_yr, psi_zy, psi_rows,
    field_a, field_dx, field_dy, field_gx, field_gy,
    pops, pop_rows, pop_xs, pop_xin, pop_xyr, pop_zxr, pop_ys, pop_yr,
    pop_zs, pop_zin, pop_zy, side_sums, sent, arrived, info, info_in,
    load_sem, send_sem, recv_sem, move_send, move_recv, info_send, info_recv,
):
    normal, planes, group_z, depth, width, breadth = sizes
    groups = depth // group_z
    me_z = lax.axis_index("normal")
    me_x = lax.axis_index("plane")
    me_y = lax.axis_index("inner")

    def device(offset):
        place = {}
        if offset[0] % normal:
            place["normal"] = lax.rem(me_z + offset[0] % normal, normal)
        if offset[1] % planes:
            place["plane"] = lax.rem(me_x + offset[1] % planes, planes)
        if offset[2] % 2:
            place["inner"] = 1 - me_y
        return place

    around = [
        (1, 1, 0), (-1, 1, 0), (1, -1, 0), (-1, -1, 0),
        (0, 1, 0), (0, -1, 0), (0, 1, 1), (0, -1, 1),
        (1, 0, 0), (-1, 0, 0), (1, 0, 1), (-1, 0, 1), (0, 0, 1),
    ]
    partners = []
    for a, b, c in around + [(0, k, 0) for k in range(1, planes)]:
        offset = (a % normal, b % planes, c % 2)
        if offset not in partners:
            partners.append(offset)
    loads = [
        pltpu.make_async_copy(source, target, load_sem.at[number])
        for number, (source, target) in enumerate(
            ((phase_hbm, phase), (velocity_hbm, velocity), (stress_hbm, stress),
             (new_slot_hbm, new_slot))
        )
    ]
    for load in loads:
        load.start()
    barrier = pltpu.get_barrier_semaphore()
    for offset in partners:
        pl.semaphore_signal(barrier, inc=1, device_id=device(offset), device_id_type=MESH)

    lane = lax.broadcasted_iota(jnp.int32, (width, breadth), 1)
    row = lax.broadcasted_iota(jnp.int32, (width, breadth), 0)
    last = breadth - 1

    def start(kind, step, pairs):
        copies = []
        for number, (offset, (source, target)) in enumerate(zip(around, pairs)):
            copy = pltpu.make_async_remote_copy(
                src_ref=source,
                dst_ref=target,
                send_sem=send_sem.at[kind, step, number],
                recv_sem=recv_sem.at[kind, step, number],
                device_id=device(offset),
                device_id_type=MESH,
            )
            copy.start()
            copies.append(copy)
        return copies

    def from_low_x(value, edge):
        return jnp.where(row == 0, edge, pltpu.roll(value, 1, 0))

    def from_high_x(value, edge):
        return jnp.where(row == width - 1, edge, pltpu.roll(value, width - 1, 0))

    def initial(z, carry):
        density = moments[0, z]
        speed = [velocity[a, z] for a in range(3)]
        momentum = [density * s for s in speed]
        for a in range(3):
            moments[1 + a, z] = momentum[a]
            speeds[a, z] = speed[a]
        for k, (a, b) in enumerate(pair_list):
            moments[4 + k, z] = momentum[a] * speed[b] + 0.375 * stress[k, z]
        return carry

    def prepare(z, carry):
        density = moments[0, z]
        inverse = 1.0 / density
        momentum = [moments[1 + a, z] for a in range(3)]
        speed = [m * inverse for m in momentum]
        eighth = 0.125 * density
        for a in range(3):
            speeds[a, z] = speed[a]
        for k, (a, b) in enumerate(pair_list):
            value = 0.625 * (momentum[a] * speed[b]) + 0.375 * moments[4 + k, z]
            moments[4 + k, z] = value - eighth if a == b else value
        return carry

    def start_density(z, carry):
        moments[0, z] = jnp.where(phase[z] == 1, 2.0, 0.3).astype(jnp.float32)
        return carry

    loads[0].wait()
    lax.fori_loop(0, depth, start_density, 0, unroll=8)

    tile = 16
    capacity = tile // group_z
    info_copies = []

    def plan():
        slots = planes * tile
        blocks = [new_slot[x] for x in range(width)]
        owners = [lax.div(block, width) for block in blocks]
        places = [lax.rem(block, width) for block in blocks]
        at_slot = []
        for x in range(width):
            earlier = jnp.int32(0)
            for other in range(x):
                earlier = earlier + jnp.where(owners[other] == owners[x], 1, 0)
            at_slot.append(owners[x] * capacity + earlier)
        shape = (slots, group_z * width)
        to_slot = lax.broadcasted_iota(jnp.int32, shape, 0)
        from_cell = lax.broadcasted_iota(jnp.int32, shape, 1)
        from_x = lax.rem(from_cell[0:8], width)
        slot_of = jnp.zeros(from_x.shape, jnp.int32)
        for x in range(width):
            slot_of = jnp.where(from_x == x, at_slot[x], slot_of)
        here = lax.div(to_slot, tile) * capacity + lax.rem(to_slot, capacity)
        layer = lax.div(lax.rem(to_slot, tile), capacity)
        chosen = (slot_of[0:1] == here) & (layer == lax.div(from_cell, width))
        order = jnp.where(chosen, 1.0, 0.0).astype(jnp.bfloat16)
        small = lax.broadcasted_iota(jnp.int32, (8, 128), 1)
        for t in range(planes):
            wanted = lax.rem(small, capacity) + t * capacity
            place = jnp.full((8, 128), -1, jnp.int32)
            for x in range(width):
                place = jnp.where(wanted == at_slot[x], places[x], place)
            info[t] = place.astype(jnp.float32)
        return order

    def send_info():
        for k in range(1, planes):
            copy = pltpu.make_async_remote_copy(
                src_ref=info.at[lax.rem(me_x + k, planes)],
                dst_ref=info_in.at[k],
                send_sem=info_send.at[k],
                recv_sem=info_recv.at[k],
                device_id=device((0, k, 0)),
                device_id_type=MESH,
            )
            copy.start()
            info_copies.append(copy)

    loads[3].wait()
    order = plan()
    started = []
    for step in range(STEPS):
        def potential(z, packed):
            value = 1.0 - jnp.exp(-moments[0, z])
            psi[step, z + 1] = value
            psi_xs[step, 0, pl.ds(z, 1), :] = value[width - 1 : width]
            psi_xs[step, 1, pl.ds(z, 1), :] = value[0:1]
            packed = jnp.where(lane == z + 17, pltpu.roll(value, z + 18, 1), packed)
            return jnp.where(lane == z + 65, pltpu.roll(value, z + 65, 1), packed)

        psi_ys[step] = lax.fori_loop(
            0, depth, potential, jnp.zeros((width, breadth), jnp.float32), unroll=16
        )
        low, high = pl.ds(0, PAD), pl.ds(depth - PAD, PAD)
        inner_rows = pl.ds(PAD, depth)
        before, after = pl.ds(0, PAD), pl.ds(depth + PAD, PAD)
        if step == 0:
            pl.semaphore_wait(barrier, len(partners))
        copies = start(0, step, [
            (psi_xs.at[step, 0, high], psi_xr.at[step, 0, before]),
            (psi_xs.at[step, 0, low], psi_xr.at[step, 0, after]),
            (psi_xs.at[step, 1, high], psi_xr.at[step, 1, before]),
            (psi_xs.at[step, 1, low], psi_xr.at[step, 1, after]),
            (psi_xs.at[step, 0], psi_xr.at[step, 0, inner_rows]),
            (psi_xs.at[step, 1], psi_xr.at[step, 1, inner_rows]),
            (psi_xs.at[step, 0], psi_xyr.at[step, 0, inner_rows]),
            (psi_xs.at[step, 1], psi_xyr.at[step, 1, inner_rows]),
            (psi.at[step, depth], psi.at[step, 0]),
            (psi.at[step, 1], psi.at[step, depth + 1]),
            (psi.at[step, depth], psi_zy.at[step, 0]),
            (psi.at[step, 1], psi_zy.at[step, 1]),
            (psi_ys.at[step], psi_yr.at[step]),
        ])
        if step == 0:
            send_info()
            loads[1].wait()
            loads[2].wait()
            lax.fori_loop(0, depth, initial, 0, unroll=4)
        else:
            lax.fori_loop(0, depth, prepare, 0, unroll=4)
        for copy in copies:
            copy.wait_recv()
        started.extend(copies)
        columns = psi_yr[step]
        for side, z_at in ((0, 16), (1, 17 + depth)):
            plane_in = psi_zy[step, side]
            columns = jnp.where(lane == z_at, pltpu.roll(plane_in, z_at + 1, 1), columns)
            columns = jnp.where(lane == z_at + 48, pltpu.roll(plane_in, z_at + 48, 1), columns)
        psi_yr[step] = columns
        rows_lane = lax.broadcasted_iota(jnp.int32, (depth + 2 * PAD, breadth), 1)
        for side in range(2):
            own, other = psi_xr[step, side], psi_xyr[step, side]
            psi_rows[0, side] = pltpu.roll(jnp.where(rows_lane == last, other, own), 1, 1)
            psi_rows[1, side] = pltpu.roll(jnp.where(rows_lane == 0, other, own), last, 1)

        def differences(p, carry):
            value = psi[step, p]
            columns = psi_yr[step]
            at = pl.ds(p + PAD - 1, 1)
            y_low = jnp.where(
                lane == 0, pltpu.roll(columns, 112 - p, 1), pltpu.roll(value, 1, 1)
            )
            y_high = jnp.where(
                lane == last, pltpu.roll(columns, 63 - p, 1), pltpu.roll(value, last, 1)
            )
            y_sum, y_diff = y_high + y_low, y_high - y_low
            x_low = from_low_x(value, psi_xr[step, 0, at, :])
            x_high = from_high_x(value, psi_xr[step, 1, at, :])
            edges = [
                [psi_rows[s, side, at, :] for s in range(2)] for side in range(2)
            ]
            x_diff = x_high - x_low
            field_a[p] = 2.0 * value + (x_high + x_low) + y_sum
            field_dx[p] = x_diff
            field_dy[p] = y_diff
            field_gx[p] = (
                2.0 * x_diff
                + from_high_x(y_sum, edges[1][1] + edges[1][0])
                - from_low_x(y_sum, edges[0][1] + edges[0][0])
            )
            field_gy[p] = (
                2.0 * y_diff
                + from_high_x(y_diff, edges[1][1] - edges[1][0])
                + from_low_x(y_diff, edges[0][1] - edges[0][0])
            )
            return carry

        lax.fori_loop(0, depth + 2, differences, 0, unroll=6)

        def collide(z, packs):
            p = z + 1
            scale = (coupling / 36.0) * psi[step, p]
            force = [
                scale * (field_a[p + 1] - field_a[p - 1]),
                scale * (field_gx[p] + (field_dx[p + 1] + field_dx[p - 1])),
                scale * (field_gy[p] + (field_dy[p + 1] + field_dy[p - 1])),
            ]
            density = moments[0, z]
            momentum = [moments[1 + a, z] for a in range(3)]
            speed = [speeds[a, z] for a in range(3)]
            post = [m + f for m, f in zip(momentum, force)]
            second = {}
            for k, (a, b) in enumerate(pair_list):
                value = moments[4 + k, z] + (speed[a] * force[b] + force[a] * speed[b])
                second[a, b] = value * (0.125 if a == b else 0.25)
            flow = [m * (1.0 / 12.0) for m in post]
            base = density * (1.0 / 36.0) - (
                second[0, 0] + second[1, 1] + second[2, 2]
            ) * (1.0 / 3.0)
            value_of = {(0, 0, 0): 12.0 * base}
            for a in range(3):
                even = 2.0 * (base + second[a, a])
                odd = 2.0 * flow[a]
                for sign in (1, -1):
                    vector = [0, 0, 0]
                    vector[a] = sign
                    value_of[tuple(vector)] = even + odd if sign == 1 else even - odd
            for a, b in pair_list[3:]:
                both = base + (second[a, a] + second[b, b])
                for sign in (1, -1):
                    if sign == 1:
                        even, odd = both + second[a, b], flow[a] + flow[b]
                    else:
                        even, odd = both - second[a, b], flow[a] - flow[b]
                    vector = [0, 0, 0]
                    vector[a], vector[b] = 1, sign
                    value_of[tuple(vector)] = even + odd
                    vector[a], vector[b] = -1, -sign
                    value_of[tuple(vector)] = even - odd
            for index, vector in enumerate(vectors):
                pops[step, index, p] = value_of[vector]
            for k in range(5):
                pop_rows[0, k, pl.ds(z, 1), :] = value_of[x_lists[0][k]][width - 1 : width]
                pop_rows[1, k, pl.ds(z, 1), :] = value_of[x_lists[1][k]][0:1]
            up, down = packs
            for k in range(5):
                at = p + 18 * k
                up = jnp.where(lane == at, pltpu.roll(value_of[y_lists[0][k]], at + 1, 1), up)
                down = jnp.where(lane == at, pltpu.roll(value_of[y_lists[1][k]], at, 1), down)
            return up, down

        nothing = jnp.zeros((width, breadth), jnp.float32)
        up, down = lax.fori_loop(0, depth, collide, (nothing, nothing), unroll=8)
        pop_ys[step, 0] = up
        pop_ys[step, 1] = down
        for k in range(5):
            pop_zs[step, 0, k] = pops[step, k, depth].astype(jnp.bfloat16)
            pop_zs[step, 1, k] = pops[step, 5 + k, 1].astype(jnp.bfloat16)
            for side in range(2):
                pop_xs[step, side, k] = pop_rows[side, k].astype(jnp.bfloat16)
        two = pl.ds(3, 2)
        copies = start(1, step, [
            (pop_xs.at[step, 0, 1], pop_zxr.at[step, 0, 0]),
            (pop_xs.at[step, 0, 2], pop_zxr.at[step, 0, 1]),
            (pop_xs.at[step, 1, 1], pop_zxr.at[step, 1, 0]),
            (pop_xs.at[step, 1, 2], pop_zxr.at[step, 1, 1]),
            (pop_xs.at[step, 0], pop_xin.at[step, 0]),
            (pop_xs.at[step, 1], pop_xin.at[step, 1]),
            (pop_xs.at[step, 0, two], pop_xyr.at[step, 0]),
            (pop_xs.at[step, 1, two], pop_xyr.at[step, 1]),
            (pop_zs.at[step, 0], pop_zin.at[step, 0]),
            (pop_zs.at[step, 1], pop_zin.at[step, 1]),
            (pop_zs.at[step, 0, two], pop_zy.at[step, 0]),
            (pop_zs.at[step, 1, two], pop_zy.at[step, 1]),
            (pop_ys.at[step], pop_yr.at[step]),
        ])

        def stream(z, carry):
            up, down = pop_yr[step, 0], pop_yr[step, 1]
            passed = {}
            for index, vector in enumerate(vectors):
                p = z + 1 - vector[0]
                value = pops[step, index, p]
                if vector[2] == 1:
                    at = p + 18 * y_lists[0].index(vector)
                    value = jnp.where(
                        lane == 0, pltpu.roll(up, 128 - at, 1), pltpu.roll(value, 1, 1)
                    )
                elif vector[2] == -1:
                    at = p + 18 * y_lists[1].index(vector)
                    value = jnp.where(
                        lane == last, pltpu.roll(down, 127 - at, 1), pltpu.roll(value, last, 1)
                    )
                if vector[1] == 1:
                    value = from_low_x(value, 0.0)
                elif vector[1] == -1:
                    value = from_high_x(value, 0.0)
                passed[vector] = value
            totals, moved = {}, {}
            for a in range(3):
                vector = [0, 0, 0]
                vector[a] = 1
                plus = passed[tuple(vector)]
                vector[a] = -1
                minus = passed[tuple(vector)]
                totals[a], moved[a] = plus + minus, plus - minus
            axis_sum = totals[0] + totals[1] + totals[2]
            cross, pair_sum = {}, {}
            for a, b in pair_list[3:]:
                found = {}
                for sign_a in (1, -1):
                    for sign_b in (1, -1):
                        vector = [0, 0, 0]
                        vector[a], vector[b] = sign_a, sign_b
                        found[sign_a, sign_b] = passed[tuple(vector)]
                same = found[1, 1] + found[-1, -1]
                mixed = found[1, -1] + found[-1, 1]
                same_odd = found[1, 1] - found[-1, -1]
                mixed_odd = found[1, -1] - found[-1, 1]
                cross[a, b] = same - mixed
                pair_sum[a, b] = same + mixed
                moved[a] = moved[a] + (same_odd + mixed_odd)
                moved[b] = moved[b] + (same_odd - mixed_odd)
            moments[0, z] = passed[0, 0, 0] + axis_sum + (
                pair_sum[0, 1] + pair_sum[0, 2] + pair_sum[1, 2]
            )
            for a in range(3):
                moments[1 + a, z] = moved[a]
            moments[4, z] = totals[0] + (pair_sum[0, 1] + pair_sum[0, 2])
            moments[5, z] = totals[1] + (pair_sum[0, 1] + pair_sum[1, 2])
            moments[6, z] = totals[2] + (pair_sum[0, 2] + pair_sum[1, 2])
            for k, pair in enumerate(pair_list[3:]):
                moments[7 + k, z] = cross[pair]
            return carry

        copies[-1].wait_recv()
        lax.fori_loop(1, depth - 1, stream, 0, unroll=7)
        for copy in copies[:-1]:
            copy.wait_recv()
        started.extend(copies)
        f32 = jnp.float32
        for k in range(5):
            pops[step, k, 0] = pop_zin[step, 0, k].astype(f32)
            pops[step, 5 + k, depth + 1] = pop_zin[step, 1, k].astype(f32)
        far = 36 + depth + 1
        corner = [[pop_zy[step, side, k].astype(f32) for k in range(2)] for side in range(2)]
        up, down = pop_yr[step, 0], pop_yr[step, 1]
        up = jnp.where(lane == 18, pltpu.roll(corner[0][0], 19, 1), up)
        down = jnp.where(lane == 18, pltpu.roll(corner[0][1], 18, 1), down)
        up = jnp.where(lane == far, pltpu.roll(corner[1][0], far + 1, 1), up)
        down = jnp.where(lane == far, pltpu.roll(corner[1][1], far, 1), down)
        pop_yr[step, 0] = up
        pop_yr[step, 1] = down
        lax.fori_loop(0, 2, lambda i, carry: stream(i * (depth - 1), carry), 0, unroll=2)

        z_row = lax.broadcasted_iota(jnp.int32, (depth, breadth), 0)
        z_lane = lax.broadcasted_iota(jnp.int32, (depth, breadth), 1)
        for side in range(2):
            own = [pop_xin[step, side, k].astype(f32) for k in range(5)]
            edge = [pop_zxr[step, side, k].astype(f32) for k in range(2)]
            other = [pop_xyr[step, side, k].astype(f32) for k in range(2)]
            plain = own[0]
            z_up = jnp.where(z_row == 0, pltpu.roll(edge[0], 1, 0), pltpu.roll(own[1], 1, 0))
            z_down = jnp.where(
                z_row == depth - 1,
                pltpu.roll(edge[1], depth - 1, 0),
                pltpu.roll(own[2], depth - 1, 0),
            )
            y_up = pltpu.roll(jnp.where(z_lane == last, other[0], own[3]), 1, 1)
            y_down = pltpu.roll(jnp.where(z_lane == 0, other[1], own[4]), last, 1)
            z_even, z_odd = z_up + z_down, z_up - z_down
            y_even, y_odd = y_up + y_down, y_up - y_down
            total = plain + (z_even + y_even)
            if side == 0:
                adds = [total, z_odd, total, y_odd, z_even, total, y_even, z_odd, y_odd]
            else:
                adds = [total, z_odd, -total, y_odd, z_even, total, y_even, -z_odd, -y_odd]
            for k, add in enumerate(adds):
                side_sums[side, k] = add

        def add_sides(z, carry):
            at = pl.ds(z, 1)
            for k, c in enumerate((0, 1, 2, 3, 4, 5, 6, 7, 9)):
                for side, x in ((0, 0), (1, width - 1)):
                    cells = (c, z, pl.ds(x, 1), slice(None))
                    moments[cells] = moments[cells] + side_sums[side, k, at, :]
            return carry

        if step < STEPS - 1:
            lax.fori_loop(0, depth, add_sides, 0, unroll=4)

    moves = []
    for g in range(groups):
        lax.fori_loop(g * group_z, (g + 1) * group_z, add_sides, 0, unroll=4)
        block = jnp.concatenate(
            [
                moments[c, g * group_z : (g + 1) * group_z]
                .reshape(group_z * width, breadth)
                .astype(jnp.bfloat16)
                for c in range(10)
            ],
            axis=1,
        )
        rows = jnp.dot(order, block, preferred_element_type=jnp.float32).astype(jnp.bfloat16)
        for c in range(10):
            sent[g, :, c] = rows[:, c * breadth : (c + 1) * breadth].reshape(
                planes, tile, breadth
            )
        for k in range(planes - 1, 0, -1):
            copy = pltpu.make_async_remote_copy(
                src_ref=sent.at[g, lax.rem(me_x + k, planes)],
                dst_ref=arrived.at[g, k],
                send_sem=move_send.at[g, k],
                recv_sem=move_recv.at[g, k],
                device_id=device((0, k, 0)),
                device_id_type=MESH,
            )
            copy.start()
            moves.append((g, copy))
        arrived[g, 0] = sent[g, me_x]

    for copy in started:
        copy.wait_send()

    for copy in info_copies:
        copy.wait()
    slots = planes * tile
    parts = [info[me_x, 0:1, 0:tile]]
    for k in range(1, planes):
        parts.append(info_in[k, 0:1, 0:tile])
    place = jnp.concatenate(parts, axis=1)
    to_row = lax.broadcasted_iota(jnp.int32, (group_z * width, slots), 0)
    from_slot = lax.broadcasted_iota(jnp.int32, (group_z * width, slots), 1)
    fits = (place == lax.rem(to_row, width).astype(jnp.float32)) & (
        lax.rem(from_slot, tile) // capacity == to_row // width
    )
    placing = jnp.where(fits, 1.0, 0.0).astype(jnp.bfloat16)
    for g in range(groups):
        for held, copy in moves:
            if held == g:
                copy.wait()

        block = jnp.concatenate(
            [arrived[g, :, c].reshape(slots, breadth) for c in range(10)], axis=1
        )
        rows = jnp.dot(placing, block, preferred_element_type=jnp.float32).astype(jnp.bfloat16)
        for c in range(10):
            out[c, pl.ds(g * group_z, group_z)] = rows[
                :, c * breadth : (c + 1) * breadth
            ].reshape(group_z, width, breadth)


def shards(mesh_sizes, phase, velocity, stress, new_slot):
    normal, planes = mesh_sizes
    depth, width, breadth = phase.shape
    capacity = 2 * ((width // 2 + planes - 1) // planes)
    group_z = 16 // capacity
    groups = depth // group_z
    plane = (width, breadth)
    padded = (depth + 2 * PAD, breadth)
    f32, bf16 = jnp.float32, jnp.bfloat16
    vmem = pltpu.VMEM
    dma = pltpu.SemaphoreType.DMA
    whole = pl.BlockSpec(memory_space=pltpu.VMEM)
    return pl.pallas_call(
        functools.partial(kernel, (normal, planes, group_z, depth, width, breadth)),
        out_shape=jax.ShapeDtypeStruct((10, depth, width, breadth), bf16),
        in_specs=[pl.BlockSpec(memory_space=pltpu.HBM)] * 4,
        out_specs=whole,
        scratch_shapes=[
            pltpu.SMEM((width,), jnp.int32),
            vmem((depth,) + plane, jnp.int32),
            vmem((3, depth) + plane, f32),
            vmem((6, depth) + plane, f32),
            vmem((10, depth) + plane, f32),
            vmem((3, depth) + plane, f32),
            vmem((STEPS, depth + 2) + plane, f32),
            vmem((STEPS, 2, depth, breadth), f32),
            vmem((STEPS, 2) + padded, f32),
            vmem((STEPS, 2) + padded, f32),
            vmem((STEPS,) + plane, f32),
            vmem((STEPS,) + plane, f32),
            vmem((STEPS, 2) + plane, f32),
            vmem((2, 2) + padded, f32),
        ]
        + [vmem((depth + 2,) + plane, f32)] * 5
        + [
            vmem((STEPS, 19, depth + 2) + plane, f32),
            vmem((2, 5, depth, breadth), f32),
            vmem((STEPS, 2, 5, depth, breadth), bf16),
            vmem((STEPS, 2, 5, depth, breadth), bf16),
            vmem((STEPS, 2, 2, depth, breadth), bf16),
            vmem((STEPS, 2, 2, depth, breadth), bf16),
            vmem((STEPS, 2) + plane, f32),
            vmem((STEPS, 2) + plane, f32),
            vmem((STEPS, 2, 5) + plane, bf16),
            vmem((STEPS, 2, 5) + plane, bf16),
            vmem((STEPS, 2, 2) + plane, bf16),
            vmem((2, 9, depth, breadth), f32),
            vmem((groups, planes, 10, 16, breadth), bf16),
            vmem((groups, planes, 10, 16, breadth), bf16),
            vmem((planes, 8, 128), f32),
            vmem((planes, 8, 128), f32),
            dma((4,)),
            dma((2, STEPS, 13)),
            dma((2, STEPS, 13)),
            dma((groups, planes)),
            dma((groups, planes)),
            dma((planes,)),
            dma((planes,)),
        ],
        compiler_params=pltpu.CompilerParams(
            collective_id=0, has_side_effects=True, vmem_limit_bytes=40 * 1024 * 1024
        ),
    )(*(pltpu.with_memory_space_constraint(x, pltpu.HBM) for x in (phase, velocity, stress, new_slot)))


def solution(mesh):
    placed = (
        P(("groups", "normal"), "plane", "inner"),
        P(None, ("groups", "normal"), "plane", "inner"),
        P(None, ("groups", "normal"), "plane", "inner"),
        P(("groups", "plane")),
    )
    return jax.shard_map(
        functools.partial(shards, (mesh.shape["normal"], mesh.shape["plane"])),
        mesh=mesh,
        in_specs=placed,
        out_specs=P(None, ("groups", "normal"), "plane", "inner"),
        check_vma=False,
    )
```
